128 devices in a mesh: vp: 32 (over z, x, core), cd: 4 (over y).
Axes of the slice: x: 4, y: 4, z: 4, core: 2. Of those that a mesh axis runs over, the one named last changes fastest.
Arguments:
- amplitudes: bfloat16 [64, 65536], P('vp'), may hold values from -6 to 6
- integrals: bfloat16 [131072, 8192], P(('vp', 'cd')), may hold values from -0.046875 to 0.046875
- occ_irrep: int32 [200], replicated, may hold values from 0 to 3
- pair_occ: int32 [64, 2], replicated, may hold values from 0 to 199
- cd_sector: int32 [512], replicated, may hold values from 0 to 3
- ab_sector: int32 [64], replicated, may hold values from 0 to 3, as said below
- block_owner: int32 [512, 1], replicated, may hold values from 0 to 127; in each aligned block of 512 rows (0 to 511, 512 to 1023, ...) at most 8 rows name the same one
Outputs:
- residual: float32 [64, 8192], P('vp', 'cd')
The draws below stay inside these ranges and needn't reach their ends.
Inputs may be any that keep to these rules, and one draw needn't show every extreme that they name: `block_owner`: each owner index owns at most 8 blocks and at least one; some index owns exactly 8. `ab_sector`: each ab panel of 2048 pairs holds exactly 4 blocks of each of the four sectors.
All inputs are finite; a program needn't handle non-finite values.
Results may differ from the reference program's by a relative error of at most 0.0003.
Values may be sent and summed in bfloat16 or wider, within the bound.
No kernel may reach another device: no remote copies, remote signals or barrier semaphores. Data moves between devices by JAX's collectives and lax.ppermute only.
A program may use at most 64 MiB of HBM per device.

```python
import math
import jax
import jax.numpy as jnp
import numpy as np
from jax import lax

NO = 200
IJ = 64
BLK = 128
ABP = 2048
SLOTS = 8
DEVICES_ALL = 128
NBLK = 512
NCD = 65536
AB = 8192
N_VP = 32
N_CD = 4


def draw_ab_sector(key, part):
    key = jax.random.fold_in(key, 5)
    panel_blocks = ABP // BLK
    panel_total = AB // ABP
    base = (jnp.arange(panel_blocks, dtype=jnp.int32) % 4).astype(jnp.int32)
    panel_keys = jax.random.split(key, panel_total)
    shuffled = jax.vmap(lambda single: jax.random.permutation(single, base))(panel_keys)
    return shuffled.reshape(panel_total * panel_blocks).astype(jnp.int32)


def place_ends(values, stream_key, least, largest):
    dims = values.shape
    place = [jax.random.randint(jax.random.fold_in(stream_key, axis), (), 0, dims[axis]) for axis in range(len(dims))]
    values = values.at[tuple(place)].set(least)
    longest = dims.index(max(dims))
    place[longest] = (place[longest] + 1) % dims[longest]
    return values.at[tuple(place)].set(largest)


def steps_of(key, shape, cuts, low, largest):
    def one(axis_at, blocks):
        steps = jax.random.uniform(jax.random.fold_in(jax.random.fold_in(key, 6), axis_at), (blocks,), jnp.float32, low / len(cuts), largest / len(cuts))
        return jnp.repeat(jnp.exp(steps), shape[axis_at] // blocks).reshape((-1,) + (1,) * (len(shape) - axis_at - 1))

    loudness = one(*cuts[0])
    for cut in cuts[1:]:
        loudness = loudness * one(*cut)
    return loudness


def shared_out(stream_key, own, number, rows, count, top, reach, slope):
    order = jax.random.permutation(stream_key, count)
    packed, usual = portions_of(count, rows * top, reach, slope, True), portions_of(count, rows * top, reach, slope, False)
    places = jnp.arange(count)

    def named(sizes, rotation):
        used = int((sizes > 0).sum())
        fixed = max(1, used // 4)
        passed = fixed + (places - fixed + rotation * (used - fixed)) % max(1, count - fixed)
        return jnp.zeros((count,), jnp.int32).at[order[jnp.where(places < fixed, places, passed)]].set(jnp.asarray(sizes, jnp.int32))

    sizes = jnp.where(number % 4 == 0, named(packed, number // 4), named(usual, number - number // 4 - 1))
    mixed = jax.random.permutation(jax.random.fold_in(own, 3), count)
    donor, taker = mixed[0:count // 2 * 2:2], mixed[1:count // 2 * 2:2]
    slack = jnp.minimum(sizes[donor] - 1, reach - sizes[taker]) // 2
    slack = jnp.where((donor == order[0]) | (taker == order[0]) | (sizes[taker] == 0), 0, jnp.maximum(slack, 0))
    passed = jax.random.randint(jax.random.fold_in(own, 4), (count // 2,), 0, 1 << 20) % (slack + 1)
    sizes = sizes.at[donor].add(-passed).at[taker].add(passed)
    items = jnp.searchsorted(jnp.cumsum(sizes), jnp.arange(rows * top), side="right").astype(jnp.int32)
    table = items.reshape(top, rows).T
    table = table[jax.random.permutation(jax.random.fold_in(own, 1), rows)]
    rotation = jax.random.randint(jax.random.fold_in(own, 2), (rows, 1), 0, top)
    return jnp.take_along_axis(table, (jnp.arange(top)[None, :] + rotation) % top, axis=1)


def portions_of(number_of, total, reach, lean, full):
    portions = [(1 << 20) // math.isqrt(rank ** lean) + 1 for rank in range(1, number_of + 1)]
    largest = reach if full else min(reach, max(-(-total // number_of), total * portions[0] // sum(portions)))
    least = 1 if total - largest >= number_of - 1 else 0
    counts, surplus = [largest] + [least] * (number_of - 1), total - largest - least * (number_of - 1)
    while surplus > 0:
        free = [i for i in range(1, number_of) if counts[i] < largest] or [i for i in range(1, number_of) if counts[i] < reach]
        whole, remaining = sum([portions[i] for i in free]), surplus
        for i in free:
            more = min(reach - counts[i], max(1, remaining * portions[i] // whole), surplus)
            counts[i] = counts[i] + more
            surplus = surplus - more
    return np.array(counts)


def noise(rng, extent, deviation, bound, cuts=(), kind=jnp.bfloat16):
    loudness = steps_of(rng, extent, cuts, -0.22, 0.18) if cuts else 1.0
    values = jax.random.normal(rng, extent, jnp.float32) * deviation * loudness
    return jnp.minimum(jnp.maximum(values, -bound), bound).astype(kind)


def setup_inputs(seed: int = 0) -> dict:
    keys = jax.random.split(jax.random.key(seed), 8)
    amplitudes = noise(keys[0], (IJ, NCD), 1.0, 6.0, ((0, 32),))
    integrals = noise(keys[1], (DEVICES_ALL * SLOTS * BLK, AB), (NCD // 4) ** -0.5, 0.046875, ((0, 128),))
    occ_irrep = place_ends(jax.random.randint(keys[2], (NO,), 0, 4), jax.random.fold_in(keys[2], 1), 0, 3).astype(jnp.int32)
    pair_occ = place_ends(jax.random.randint(keys[3], (IJ, 2), 0, NO), jax.random.fold_in(keys[3], 1), 0, NO - 1).astype(jnp.int32)
    cd_sector = place_ends(jax.random.randint(keys[4], (NBLK,), 0, 4), jax.random.fold_in(keys[4], 1), 0, 3).astype(jnp.int32)
    ab_sector = draw_ab_sector(jax.random.fold_in(keys[7], 71), 0)
    block_owner_keys = jax.random.split(jax.random.fold_in(keys[6], 1), NBLK // NBLK)
    block_owner_turns = jax.random.permutation(jax.random.fold_in(keys[6], 3), NBLK // NBLK)
    block_owner = jax.vmap(lambda own, number: shared_out(jax.random.fold_in(keys[6], 2), own, number, NBLK, DEVICES_ALL, 1, SLOTS, 1))(block_owner_keys, block_owner_turns).reshape((NBLK, 1))
    return {"amplitudes": amplitudes, "integrals": integrals, "occ_irrep": occ_irrep, "pair_occ": pair_occ, "cd_sector": cd_sector, "ab_sector": ab_sector, "block_owner": block_owner}


def pair_symmetry(occ_irrep, pair_occ):
    orbitals = jnp.arange(occ_irrep.shape[0], dtype=jnp.int32)
    first = jnp.sum(jnp.where(pair_occ[:, 0:1] == orbitals[None, :], occ_irrep[None, :], 0), axis=1)
    second = jnp.sum(jnp.where(pair_occ[:, 1:2] == orbitals[None, :], occ_irrep[None, :], 0), axis=1)
    return jnp.bitwise_xor(first, second).astype(jnp.int32)


def slot_positions(block_owner, device_total, slot_count):
    owners = block_owner[:, 0]
    owner_hot = (owners[:, None] == jnp.arange(device_total, dtype=jnp.int32)[None, :]).astype(jnp.int32)
    earlier = jnp.cumsum(owner_hot, axis=0) - owner_hot
    block_rank = jnp.sum(earlier * owner_hot, axis=1)
    return (owners * slot_count + block_rank).astype(jnp.int32)


def reference(amplitudes, integrals, occ_irrep, pair_occ, cd_sector, ab_sector, block_owner):
    device_total = N_VP * N_CD
    pair_sym = pair_symmetry(occ_irrep, pair_occ)
    position = slot_positions(block_owner, device_total, SLOTS)
    allowed = cd_sector[None, :] == pair_sym[:, None]
    blocked = amplitudes.reshape(IJ, NBLK, BLK)
    masked = jnp.where(allowed[:, :, None], blocked, jnp.zeros_like(blocked))
    placed = jnp.zeros((IJ, device_total * SLOTS, BLK), amplitudes.dtype).at[:, position, :].set(masked)
    placed = jnp.transpose(placed.reshape(IJ, device_total, SLOTS * BLK), (1, 0, 2))
    slabs = integrals.reshape(device_total, SLOTS * BLK, AB)

    def accumulate(running, pieces):
        return running + jnp.dot(pieces[0], pieces[1], preferred_element_type=jnp.float32), None

    total, _ = lax.scan(accumulate, jnp.zeros((IJ, AB), jnp.float32), (placed, slabs))
    ab_columns = jnp.repeat(ab_sector, BLK, total_repeat_length=AB)
    return jnp.where(pair_sym[:, None] == ab_columns[None, :], total, jnp.zeros_like(total))
```

```python
import jax
import jax.numpy as jnp
from jax import lax
from jax.experimental import pallas as pl
from jax.experimental.pallas import tpu as pltpu
from jax.sharding import PartitionSpec as P

BLK = 128
F32 = jnp.float32
BF16 = jnp.bfloat16


def iota(shape, dim):
    return lax.broadcasted_iota(jnp.int32, shape, dim)


def ones_where(mask):
    return jnp.where(mask, 1.0, 0.0).astype(BF16)


def dot(a, b):
    return jnp.dot(a, b, preferred_element_type=F32)


def row_symmetry(occ, pair, row):
    return occ[pair[0, row]] ^ occ[pair[1, row]]


def route_kernel(occ, pair, amp, owner, cd, ab, out, table):
    vp = lax.axis_index("vp")
    y = lax.axis_index("cd")
    nblk = owner.shape[1]
    sym0 = row_symmetry(occ, pair, 2 * vp)
    sym1 = row_symmetry(occ, pair, 2 * vp + 1)
    own = owner[...]
    cdrow = cd[...]
    prow = iota((48, nblk), 0)
    ids = jnp.where(prow < 32, prow, vp) * 4 + y
    hot = own == ids
    before = ones_where(iota((nblk, nblk), 0) < iota((nblk, nblk), 1))
    rank = dot(ones_where(hot), before)
    rank32 = rank[:32]
    hot32 = hot[:32]
    code0 = jnp.where(hot32 & (cdrow == sym0), rank32 * 2.0, -4.0)
    code1 = jnp.where(hot32 & (cdrow == sym1), rank32 * 2.0 + 1.0, -4.0)
    codes = jnp.concatenate([code0, code1], axis=0).astype(BF16)
    widen = ones_where(iota((nblk, 2 * nblk), 0) == (iota((nblk, 2 * nblk), 1) >> 1))
    wide = dot(codes, widen)
    code = jnp.where((iota((32, 2 * nblk), 1) & 1) == 0, wide[:32], wide[32:])
    place = iota((32, 16, 2 * nblk), 1).astype(F32)
    select = ones_where(code[:, None, :] == place).reshape(512, 2 * nblk)
    out[...] = dot(select, amp[...]).astype(BF16)
    mine = jnp.where(hot[32:33], rank[32:33], -1.0)
    at_slot = mine == iota((16, nblk), 0).astype(F32)
    sector = jnp.sum(jnp.where(at_slot, cdrow.astype(F32), 0.0), axis=1, keepdims=True)
    match = ab[...].astype(F32) == sector
    nab = ab.shape[1]
    j0 = iota((nab, nab), 0)
    j1 = iota((nab, nab), 1)
    order = dot(ones_where(match), ones_where((j0 < j1) & ((j0 >> 4) == (j1 >> 4))))
    source = iota((nab, BLK), 0)
    total = jnp.zeros((16, BLK), F32)
    for m in range(4):
        spot = iota((nab, BLK), 1) == (source >> 4) * 4 + m
        value = jnp.where(spot, source.astype(F32), 0.0).astype(BF16)
        total = total + dot(ones_where(match & (order == float(m))), value)
    table[...] = total[:8].astype(jnp.int32)


def contract_kernel(table, recv, integrals, out):
    row = iota((512, 512), 0)
    origin = (row & 31) * 16 + (row >> 6) * 2 + ((row >> 5) & 1)
    a = dot(ones_where(origin == iota((512, 512), 1)), recv[...]).astype(BF16)
    a = jnp.concatenate([a[s * 64:(s + 1) * 64] for s in range(8)], axis=1)
    for pair_at in range(8):
        columns = []
        for half in range(2):
            cb = pair_at * 2 + half
            columns.append(
                jnp.concatenate(
                    [
                        integrals[
                            s * BLK:(s + 1) * BLK,
                            pl.ds(pl.multiple_of(table[s, cb] * BLK, BLK), BLK),
                        ]
                        for s in range(8)
                    ],
                    axis=0,
                )
            )
        result = dot(a, jnp.concatenate(columns, axis=1))
        for half in range(2):
            cb = pair_at * 2 + half
            for r in range(2):
                out[pl.Slice((cb // 4) * 8 + r * 4 + cb % 4, 32, stride=32), :] = result[
                    r * 32:(r + 1) * 32, half * BLK:(half + 1) * BLK
                ]


def collect_kernel(occ, pair, ab, recv, out, total):
    vp = lax.axis_index("vp")
    y = lax.axis_index("cd")
    total[...] = jnp.sum(recv[...], axis=0)
    for r in range(2):
        sym = row_symmetry(occ, pair, 2 * vp + r)
        count = jnp.int32(0)
        for j in range(16):
            hit = ab[y * 16 + j] == sym
            line = total[pl.ds(r * 4 + jnp.minimum(count, 3), 1), :]
            out[r:r + 1, j * BLK:(j + 1) * BLK] = jnp.where(hit, line, 0.0)
            count = count + hit.astype(jnp.int32)


SMEM = pl.BlockSpec(memory_space=pltpu.SMEM)
VMEM = pl.BlockSpec(memory_space=pltpu.VMEM)


def shards(amplitudes, integrals, occ_irrep, pair_occ, cd_sector, ab_sector, block_owner):
    nblk = cd_sector.shape[0]
    amp = amplitudes.reshape(2, nblk, BLK).transpose(1, 0, 2).reshape(2 * nblk, BLK)
    pair = pair_occ.T
    outgoing, table = pl.pallas_call(
        route_kernel,
        out_shape=(
            jax.ShapeDtypeStruct((512, BLK), BF16),
            jax.ShapeDtypeStruct((8, BLK), jnp.int32),
        ),
        in_specs=[SMEM, SMEM, VMEM, VMEM, VMEM, VMEM],
        out_specs=(VMEM, VMEM),
        compiler_params=pltpu.CompilerParams(vmem_limit_bytes=16 << 20),
        name="route",
    )(occ_irrep, pair, amp, block_owner.T, cd_sector[None, :], ab_sector[None, :])
    incoming = lax.all_to_all(
        outgoing.reshape(32, 16, BLK), "vp", split_axis=0, concat_axis=0, tiled=True
    ).reshape(512, BLK)
    partial_value = pl.pallas_call(
        contract_kernel,
        out_shape=jax.ShapeDtypeStruct((1024, BLK), F32),
        in_specs=[SMEM, VMEM, VMEM],
        out_specs=VMEM,
        compiler_params=pltpu.CompilerParams(vmem_limit_bytes=28 << 20),
        name="contract",
    )(table, incoming, pltpu.with_memory_space_constraint(integrals, pltpu.VMEM))
    gathered = lax.all_to_all(
        partial_value.reshape(128, 8, BLK), ("vp", "cd"), split_axis=0, concat_axis=0, tiled=True
    )
    return pl.pallas_call(
        collect_kernel,
        out_shape=jax.ShapeDtypeStruct((2, 2048), F32),
        in_specs=[SMEM, SMEM, SMEM, VMEM],
        out_specs=VMEM,
        scratch_shapes=[pltpu.VMEM((8, BLK), F32)],
        compiler_params=pltpu.CompilerParams(vmem_limit_bytes=8 << 20),
        name="collect",
    )(occ_irrep, pair, ab_sector, gathered)


def solution(mesh):
    return jax.shard_map(
        shards,
        mesh=mesh,
        in_specs=(P("vp", None), P(("vp", "cd"), None), P(), P(), P(), P(), P()),
        out_specs=P("vp", "cd"),
        check_vma=False,
    )
```

```python
import jax
import jax.numpy as jnp
from jax import lax
from jax.experimental import pallas as pl
from jax.experimental.pallas import tpu as pltpu
from jax.sharding import PartitionSpec as P

BLK = 128
F32 = jnp.float32
BF16 = jnp.bfloat16


def iota(shape, dim):
    return lax.broadcasted_iota(jnp.int32, shape, dim)


def ones_where(mask):
    return jnp.where(mask, 1.0, 0.0).astype(BF16)


def dot(a, b):
    return jnp.dot(a, b, preferred_element_type=F32)


def row_symmetry(occ, pair, row):
    return occ[pair[0, row]] ^ occ[pair[1, row]]


def fetch(sems, *pairs):
    copies = [pltpu.make_async_copy(src, dst, sems.at[i]) for i, (src, dst) in enumerate(pairs)]
    for copy in copies:
        copy.start()
    return copies


def route_kernel(
    occ_h, pair_h, amp_h, owner_h, cd_h, ab_h, integrals, out, blocks,
    occ, pair, amp, owner, cd, ab, table_v, table, sems, row_sems,
):
    copies = fetch(
        sems, (owner_h, owner), (cd_h, cd), (ab_h, ab), (occ_h, occ), (pair_h, pair), (amp_h, amp)
    )
    vp = lax.axis_index("vp")
    y = lax.axis_index("cd")
    nblk = owner.shape[1]
    nab = ab.shape[1]
    before = ones_where(iota((nblk, nblk), 0) < iota((nblk, nblk), 1))
    widen = ones_where(iota((nblk, 2 * nblk), 0) == (iota((nblk, 2 * nblk), 1) >> 1))
    for copy in copies[:5]:
        copy.wait()
    cdrow = cd[...]
    prow = iota((48, nblk), 0)
    hot = owner[...] == jnp.where(prow < 32, prow, vp) * 4 + y
    rank = dot(ones_where(hot), before)
    mine = jnp.where(hot[32:], rank[32:], -1.0)
    at_slot = mine == iota((16, nblk), 0).astype(F32)
    sector = jnp.sum(jnp.where(at_slot, cdrow.astype(F32), 0.0), axis=1, keepdims=True)
    match = ab[...].astype(F32) == sector
    j0 = iota((nab, nab), 0)
    j1 = iota((nab, nab), 1)
    order = dot(ones_where(match), ones_where((j0 < j1) & ((j0 >> 4) == (j1 >> 4))))
    source = iota((nab, BLK), 0)
    total = jnp.zeros((16, BLK), F32)
    for m in range(4):
        spot = iota((nab, BLK), 1) == (source >> 4) * 4 + m
        value = jnp.where(spot, source.astype(F32), 0.0).astype(BF16)
        total = total + dot(ones_where(match & (order == float(m))), value)
    table_v[...] = total[:8].astype(jnp.int32)
    to_scalars = pltpu.make_async_copy(table_v, table, sems.at[0])
    to_scalars.start()
    sym0 = row_symmetry(occ, pair, 2 * vp)
    sym1 = row_symmetry(occ, pair, 2 * vp + 1)
    code0 = jnp.where(hot[:32] & (cdrow == sym0), rank[:32] * 2.0, -4.0)
    code1 = jnp.where(hot[:32] & (cdrow == sym1), rank[:32] * 2.0 + 1.0, -4.0)
    codes = jnp.concatenate([code0, code1], axis=0).astype(BF16)
    wide = dot(codes, widen)
    code = jnp.where((iota((32, 2 * nblk), 1) & 1) == 0, wide[:32], wide[32:])
    to_scalars.wait()

    for s in range(8):
        for cb in range(16):
            start = pl.multiple_of(table[s, cb] * BLK, BLK)
            pltpu.make_async_copy(
                integrals.at[s * BLK:(s + 1) * BLK, pl.ds(start, BLK)],
                blocks.at[s * BLK:(s + 1) * BLK, cb * BLK:(cb + 1) * BLK],
                row_sems.at[s],
            ).start()
    place = iota((32, 16, 2 * nblk), 1).astype(F32)
    select = ones_where(code[:, None, :] == place).reshape(512, 2 * nblk)
    copies[5].wait()
    out[...] = dot(select, amp[...]).astype(BF16)
    for s in range(8):
        rows = blocks.at[s * BLK:(s + 1) * BLK, :]
        pltpu.make_async_copy(rows, rows, row_sems.at[s]).wait()


def contract_kernel(recv, blocks, out):
    row = iota((512, 512), 0)
    origin = (row & 31) * 16 + (row >> 6) * 2 + ((row >> 5) & 1)
    a = dot(ones_where(origin == iota((512, 512), 1)), recv[...]).astype(BF16)
    a = jnp.concatenate([a[s * 64:(s + 1) * 64] for s in range(8)], axis=1)
    for pair_at in range(8):
        result = dot(a, blocks[:, pair_at * 256:(pair_at + 1) * 256])
        for half in range(2):
            cb = pair_at * 2 + half
            for r in range(2):
                out[pl.Slice((cb // 4) * 8 + r * 4 + cb % 4, 32, stride=32), :] = result[
                    r * 32:(r + 1) * 32, half * BLK:(half + 1) * BLK
                ]


def collect_kernel(occ, pair, ab, recv, out, total):
    vp = lax.axis_index("vp")
    y = lax.axis_index("cd")
    total[...] = jnp.sum(recv[...], axis=0)
    for r in range(2):
        sym = row_symmetry(occ, pair, 2 * vp + r)
        count = jnp.int32(0)
        for j in range(16):
            hit = ab[y * 16 + j] == sym
            line = total[pl.ds(r * 4 + jnp.minimum(count, 3), 1), :]
            out[r:r + 1, j * BLK:(j + 1) * BLK] = jnp.where(hit, line, 0.0)
            count = count + hit.astype(jnp.int32)


SMEM = pl.BlockSpec(memory_space=pltpu.SMEM)
VMEM = pl.BlockSpec(memory_space=pltpu.VMEM)
HBM = pl.BlockSpec(memory_space=pltpu.HBM)


def hbm(*arrays):
    return [pltpu.with_memory_space_constraint(a, pltpu.HBM) for a in arrays]


def shards(amplitudes, integrals, occ_irrep, pair_occ, cd_sector, ab_sector, block_owner):
    nblk = cd_sector.shape[0]
    amp = amplitudes.reshape(2, nblk, BLK).transpose(1, 0, 2).reshape(2 * nblk, BLK)
    pair = pair_occ.T
    owner, cd, ab = block_owner.T, cd_sector[None, :], ab_sector[None, :]
    outgoing, blocks = pl.pallas_call(
        route_kernel,
        out_shape=(
            jax.ShapeDtypeStruct((512, BLK), BF16),
            pltpu.VMEM((1024, 2048), BF16),
        ),
        in_specs=[HBM] * 7,
        out_specs=(VMEM, VMEM),
        scratch_shapes=[
            pltpu.SMEM(occ_irrep.shape, jnp.int32),
            pltpu.SMEM(pair.shape, jnp.int32),
            pltpu.VMEM(amp.shape, BF16),
            pltpu.VMEM(owner.shape, jnp.int32),
            pltpu.VMEM(cd.shape, jnp.int32),
            pltpu.VMEM(ab.shape, jnp.int32),
            pltpu.VMEM((8, BLK), jnp.int32),
            pltpu.SMEM((8, BLK), jnp.int32),
            pltpu.SemaphoreType.DMA((6,)),
            pltpu.SemaphoreType.DMA((8,)),
        ],
        compiler_params=pltpu.CompilerParams(vmem_limit_bytes=16 << 20),
        name="route",
    )(*hbm(occ_irrep, pair, amp, owner, cd, ab, integrals))
    incoming = lax.all_to_all(
        outgoing.reshape(32, 16, BLK), "vp", split_axis=0, concat_axis=0, tiled=True
    ).reshape(512, BLK)
    partial_value = pl.pallas_call(
        contract_kernel,
        out_shape=jax.ShapeDtypeStruct((1024, BLK), F32),
        in_specs=[VMEM, VMEM],
        out_specs=VMEM,
        compiler_params=pltpu.CompilerParams(vmem_limit_bytes=28 << 20),
        name="contract",
    )(incoming, pltpu.with_memory_space_constraint(blocks, pltpu.VMEM))
    gathered = lax.all_to_all(
        partial_value.reshape(128, 8, BLK), ("vp", "cd"), split_axis=0, concat_axis=0, tiled=True
    )
    return pl.pallas_call(
        collect_kernel,
        out_shape=jax.ShapeDtypeStruct((2, 2048), F32),
        in_specs=[SMEM, SMEM, SMEM, VMEM],
        out_specs=VMEM,
        scratch_shapes=[pltpu.VMEM((8, BLK), F32)],
        compiler_params=pltpu.CompilerParams(vmem_limit_bytes=8 << 20),
        name="collect",
    )(occ_irrep, pair, ab_sector, gathered)


def solution(mesh):
    return jax.shard_map(
        shards,
        mesh=mesh,
        in_specs=(P("vp", None), P(("vp", "cd"), None), P(), P(), P(), P(), P()),
        out_specs=P("vp", "cd"),
        check_vma=False,
    )
```

```python
import jax
import jax.numpy as jnp
from jax import lax
from jax.experimental import pallas as pl
from jax.experimental.pallas import tpu as pltpu
from jax.sharding import PartitionSpec as P

BLK = 128
F32 = jnp.float32
BF16 = jnp.bfloat16


def iota(shape, dim):
    return lax.broadcasted_iota(jnp.int32, shape, dim)


def ones_where(mask):
    return jnp.where(mask, 1.0, 0.0).astype(BF16)


def dot(a, b):
    return jnp.dot(a, b, preferred_element_type=F32)


def row_symmetry(occ, pair, row):
    return occ[pair[0, row]] ^ occ[pair[1, row]]


def fetch(sems, *pairs):
    copies = [pltpu.make_async_copy(src, dst, sems.at[i]) for i, (src, dst) in enumerate(pairs)]
    for copy in copies:
        copy.start()
    return copies


def route_kernel(
    occ_h, pair_h, amp_h, owner_h, cd_h, ab_h, integrals, out, blocks, spread,
    occ, pair, amp, owner, cd, ab, lists_v, lists, sems, row_sems,
):
    copies = fetch(
        sems, (owner_h, owner), (cd_h, cd), (ab_h, ab), (occ_h, occ), (pair_h, pair), (amp_h, amp)
    )
    vp = lax.axis_index("vp")
    y = lax.axis_index("cd")
    nblk = owner.shape[1]
    nab = ab.shape[1]
    half_col = iota((nblk, 2 * nblk), 1) >> 1
    before = ones_where(iota((nblk, nblk), 0) < iota((nblk, nblk), 1))
    before2 = ones_where(iota((nblk, 2 * nblk), 0) < half_col)
    widen = ones_where(iota((nblk, 2 * nblk), 0) == half_col)
    j0 = iota((nab, nab), 0)
    j1 = iota((nab, nab), 1)
    within = ones_where((j0 < j1) & ((j0 >> 4) == (j1 >> 4)))
    for copy in copies[:5]:
        copy.wait()
    own = owner[...]
    cdf = cd[...].astype(F32)
    hot = own == vp * 4 + y
    rank = dot(jnp.broadcast_to(ones_where(hot), (16, nblk)), before)[:1]
    mine = jnp.where(hot, rank, -1.0)
    sym0 = row_symmetry(occ, pair, 2 * vp)
    sym1 = row_symmetry(occ, pair, 2 * vp + 1)
    row = iota((16, 1), 0)
    wanted = jnp.where(row < 8, row, jnp.where(row < 12, sym0, sym1))
    match = ab[...] == wanted
    order = dot(ones_where(match), within)
    source = iota((nab, BLK), 0)
    total = jnp.zeros((16, BLK), F32)
    for m in range(4):
        spot = iota((nab, BLK), 1) == (source >> 4) * 4 + m
        value = jnp.where(spot, source.astype(F32), 0.0).astype(BF16)
        total = total + dot(ones_where(match & (order == float(m))), value)
    lists_v[...] = total[:8].astype(jnp.int32)
    to_scalars = pltpu.make_async_copy(lists_v, lists, sems.at[0])
    to_scalars.start()
    sector = [
        jnp.sum(jnp.where(mine == float(s), cdf, 0.0)).astype(jnp.int32) for s in range(8)
    ]
    hot32 = own == iota((32, nblk), 0) * 4 + y
    rank2 = dot(ones_where(hot32), before2)
    both = jnp.concatenate([own.astype(F32), cdf, jnp.zeros((14, nblk), F32)], axis=0)
    wide = dot(both.astype(BF16), widen)
    parity = iota((1, 2 * nblk), 1) & 1
    sym = jnp.where(parity == 0, sym0, sym1).astype(F32)
    ids = (iota((32, 1), 0) * 4 + y).astype(F32)
    keep = (wide[:1] == ids) & (wide[1:2] == sym)
    code = jnp.where(keep, rank2 * 2.0 + parity.astype(F32), -1.0)
    to_scalars.wait()
    for s in range(8):
        for cb in range(16):
            start = pl.multiple_of(lists[sector[s], cb] * BLK, BLK)
            pltpu.make_async_copy(
                integrals.at[s * BLK:(s + 1) * BLK, pl.ds(start, BLK)],
                blocks.at[s * BLK:(s + 1) * BLK, cb * BLK:(cb + 1) * BLK],
                row_sems.at[s],
            ).start()
    place = iota((32, 16, 2 * nblk), 1).astype(F32)
    select = ones_where(code[:, None, :] == place).reshape(512, 2 * nblk)
    shift = iota((nab, BLK), 0) == iota((nab, BLK), 1) + y * 16
    places = match & (order == (row & 3).astype(F32))
    spread[...] = dot(ones_where(places), ones_where(shift))[8:]
    copies[5].wait()
    out[...] = dot(select, amp[...]).astype(BF16)
    for s in range(8):
        rows = blocks.at[s * BLK:(s + 1) * BLK, :]
        pltpu.make_async_copy(rows, rows, row_sems.at[s]).wait()


def contract_kernel(recv, blocks, out, wide):
    wide[...] = recv[...].astype(F32)
    slots = []
    for s in range(8):
        rows = [wide[pl.Slice(s * 2 + r, 32, stride=16), :] for r in range(2)]
        slots.append(jnp.concatenate(rows, axis=0).astype(BF16))
    a = jnp.concatenate(slots, axis=1)
    for pair_at in range(8):
        result = dot(a, blocks[:, pair_at * 256:(pair_at + 1) * 256])
        for half in range(2):
            cb = pair_at * 2 + half
            for r in range(2):
                out[pl.Slice((cb // 4) * 8 + r * 4 + cb % 4, 32, stride=32), :] = result[
                    r * 32:(r + 1) * 32, half * BLK:(half + 1) * BLK
                ]


def collect_kernel(spread, recv, out):
    total = jnp.sum(recv[...], axis=0)
    places = spread[...]
    for j in range(16):
        line = jnp.where(places[:, j:j + 1] > 0.0, total, 0.0)
        out[0:1, j * BLK:(j + 1) * BLK] = jnp.sum(line[:4], axis=0, keepdims=True)
        out[1:2, j * BLK:(j + 1) * BLK] = jnp.sum(line[4:], axis=0, keepdims=True)


VMEM = pl.BlockSpec(memory_space=pltpu.VMEM)
HBM = pl.BlockSpec(memory_space=pltpu.HBM)


def hbm(*arrays):
    return [pltpu.with_memory_space_constraint(a, pltpu.HBM) for a in arrays]


def shards(amplitudes, integrals, occ_irrep, pair_occ, cd_sector, ab_sector, block_owner):
    nblk = cd_sector.shape[0]
    amp = amplitudes.reshape(2, nblk, BLK).transpose(1, 0, 2).reshape(2 * nblk, BLK)
    pair = pair_occ.T
    owner, cd, ab = block_owner.T, cd_sector[None, :], ab_sector[None, :]
    outgoing, blocks, spread = pl.pallas_call(
        route_kernel,
        out_shape=(
            jax.ShapeDtypeStruct((512, BLK), BF16),
            pltpu.VMEM((1024, 2048), BF16),
            jax.ShapeDtypeStruct((8, BLK), F32),
        ),
        in_specs=[HBM] * 7,
        out_specs=(VMEM, VMEM, VMEM),
        scratch_shapes=[
            pltpu.SMEM(occ_irrep.shape, jnp.int32),
            pltpu.SMEM(pair.shape, jnp.int32),
            pltpu.VMEM(amp.shape, BF16),
            pltpu.VMEM(owner.shape, jnp.int32),
            pltpu.VMEM(cd.shape, jnp.int32),
            pltpu.VMEM(ab.shape, jnp.int32),
            pltpu.VMEM((8, BLK), jnp.int32),
            pltpu.SMEM((8, BLK), jnp.int32),
            pltpu.SemaphoreType.DMA((6,)),
            pltpu.SemaphoreType.DMA((8,)),
        ],
        compiler_params=pltpu.CompilerParams(vmem_limit_bytes=16 << 20),
        name="route",
    )(*hbm(occ_irrep, pair, amp, owner, cd, ab, integrals))
    incoming = lax.all_to_all(
        outgoing.reshape(32, 16, BLK), "vp", split_axis=0, concat_axis=0, tiled=True
    ).reshape(512, BLK)
    partial_value = pl.pallas_call(
        contract_kernel,
        out_shape=jax.ShapeDtypeStruct((1024, BLK), F32),
        in_specs=[VMEM, VMEM],
        out_specs=VMEM,
        scratch_shapes=[pltpu.VMEM((512, BLK), F32)],
        compiler_params=pltpu.CompilerParams(vmem_limit_bytes=28 << 20),
        name="contract",
    )(incoming, pltpu.with_memory_space_constraint(blocks, pltpu.VMEM))
    gathered = lax.all_to_all(
        partial_value.reshape(128, 8, BLK), ("vp", "cd"), split_axis=0, concat_axis=0, tiled=True
    )
    return pl.pallas_call(
        collect_kernel,
        out_shape=jax.ShapeDtypeStruct((2, 2048), F32),
        in_specs=[VMEM, VMEM],
        out_specs=VMEM,
        compiler_params=pltpu.CompilerParams(vmem_limit_bytes=8 << 20),
        name="collect",
    )(spread, gathered)


def solution(mesh):
    return jax.shard_map(
        shards,
        mesh=mesh,
        in_specs=(P("vp", None), P(("vp", "cd"), None), P(), P(), P(), P(), P()),
        out_specs=P("vp", "cd"),
        check_vma=False,
    )
```

```python
import jax
import jax.numpy as jnp
from jax import lax
from jax.experimental import pallas as pl
from jax.experimental.pallas import tpu as pltpu
from jax.sharding import PartitionSpec as P

BLK = 128
F32 = jnp.float32
BF16 = jnp.bfloat16


def iota(shape, dim):
    return lax.broadcasted_iota(jnp.int32, shape, dim)


def ones_where(mask):
    return jnp.where(mask, 1.0, 0.0).astype(BF16)


def dot(a, b):
    return jnp.dot(a, b, preferred_element_type=F32)


def row_symmetry(occ, pair, row):
    return occ[pair[0, row]] ^ occ[pair[1, row]]


def fetch(sems, *pairs):
    copies = [pltpu.make_async_copy(src, dst, sems.at[i]) for i, (src, dst) in enumerate(pairs)]
    for copy in copies:
        copy.start()
    return copies


def route_kernel(
    occ_h, pair_h, amp_h, owner_h, cd_h, ab_h, out, table, spread,
    occ, pair, amp, owner, cd, ab, table_v, sems,
):
    copies = fetch(
        sems, (owner_h, owner), (cd_h, cd), (ab_h, ab), (occ_h, occ), (pair_h, pair), (amp_h, amp)
    )
    vp = lax.axis_index("vp")
    y = lax.axis_index("cd")
    nblk = owner.shape[1]
    nab = ab.shape[1]
    half_col = iota((nblk, 2 * nblk), 1) >> 1
    before = ones_where(iota((nblk, nblk), 0) < iota((nblk, nblk), 1))
    before2 = ones_where(iota((nblk, 2 * nblk), 0) < half_col)
    widen = ones_where(iota((nblk, 2 * nblk), 0) == half_col)
    j0 = iota((nab, nab), 0)
    j1 = iota((nab, nab), 1)
    within = ones_where((j0 < j1) & ((j0 >> 4) == (j1 >> 4)))
    for copy in copies[:5]:
        copy.wait()
    own = owner[...]
    cdf = cd[...].astype(F32)
    hot = own == vp * 4 + y
    rank = dot(jnp.broadcast_to(ones_where(hot), (16, nblk)), before)[:1]
    mine = jnp.where(hot, rank, -1.0)
    sym0 = row_symmetry(occ, pair, 2 * vp)
    sym1 = row_symmetry(occ, pair, 2 * vp + 1)
    row = iota((16, 1), 0)
    wanted = jnp.where(row < 8, row, jnp.where(row < 12, sym0, sym1))
    match = ab[...] == wanted
    order = dot(ones_where(match), within)
    source = iota((nab, BLK), 0)
    total = jnp.zeros((16, BLK), F32)
    for m in range(4):
        spot = iota((nab, BLK), 1) == (source >> 4) * 4 + m
        value = jnp.where(spot, source.astype(F32), 0.0).astype(BF16)
        total = total + dot(ones_where(match & (order == float(m))), value)
    slot = iota((8, 1), 0).astype(F32)
    sector = jnp.sum(jnp.where(mine == slot, cdf, 0.0), axis=1, keepdims=True)
    starts = jnp.zeros((8, BLK), F32)
    for t in range(4):
        starts = starts + jnp.where(sector == float(t), total[t:t + 1], 0.0)
    table_v[...] = starts.astype(jnp.int32)
    to_scalars = pltpu.make_async_copy(table_v, table, sems.at[0])
    to_scalars.start()
    hot32 = own == iota((32, nblk), 0) * 4 + y
    rank2 = dot(ones_where(hot32), before2)
    both = jnp.concatenate([own.astype(F32), cdf, jnp.zeros((14, nblk), F32)], axis=0)
    wide = dot(both.astype(BF16), widen)
    parity = iota((1, 2 * nblk), 1) & 1
    sym = jnp.where(parity == 0, sym0, sym1).astype(F32)
    ids = (iota((32, 1), 0) * 4 + y).astype(F32)
    keep = (wide[:1] == ids) & (wide[1:2] == sym)
    code = jnp.where(keep, rank2 * 2.0 + parity.astype(F32), -1.0)
    place = iota((32, 16, 2 * nblk), 1).astype(F32)
    select = ones_where(code[:, None, :] == place).reshape(512, 2 * nblk)
    shift = iota((nab, BLK), 0) == iota((nab, BLK), 1) + y * 16
    places = match & (order == (row & 3).astype(F32))
    spread[...] = dot(ones_where(places), ones_where(shift))[8:]
    copies[5].wait()
    out[...] = dot(select, amp[...]).astype(BF16)
    to_scalars.wait()


def contract_kernel(table, recv, integrals, out, wide):
    wide[...] = recv[...].astype(F32)
    slots = []
    for s in range(8):
        rows = [wide[pl.Slice(s * 2 + r, 32, stride=16), :] for r in range(2)]
        slots.append(jnp.concatenate(rows, axis=0).astype(BF16))
    a = jnp.concatenate(slots, axis=1)
    for pair_at in range(8):
        columns = []
        for cb in (pair_at * 2, pair_at * 2 + 1):
            parts = []
            for s in range(8):
                start = pl.multiple_of(table[s, cb] * BLK, BLK)
                parts.append(integrals[s * BLK:(s + 1) * BLK, pl.ds(start, BLK)])
            columns.append(jnp.concatenate(parts, axis=0))
        result = dot(a, jnp.concatenate(columns, axis=1))
        for half in range(2):
            cb = pair_at * 2 + half
            for r in range(2):
                out[pl.Slice((cb // 4) * 8 + r * 4 + cb % 4, 32, stride=32), :] = result[
                    r * 32:(r + 1) * 32, half * BLK:(half + 1) * BLK
                ]


def collect_kernel(spread, recv, out):
    total = jnp.sum(recv[...], axis=0)
    places = spread[...]
    for j in range(16):
        line = jnp.where(places[:, j:j + 1] > 0.0, total, 0.0)
        out[0:1, j * BLK:(j + 1) * BLK] = jnp.sum(line[:4], axis=0, keepdims=True)
        out[1:2, j * BLK:(j + 1) * BLK] = jnp.sum(line[4:], axis=0, keepdims=True)


VMEM = pl.BlockSpec(memory_space=pltpu.VMEM)
SMEM = pl.BlockSpec(memory_space=pltpu.SMEM)
HBM = pl.BlockSpec(memory_space=pltpu.HBM)


def hbm(*arrays):
    return [pltpu.with_memory_space_constraint(a, pltpu.HBM) for a in arrays]


def shards(amplitudes, integrals, occ_irrep, pair_occ, cd_sector, ab_sector, block_owner):
    nblk = cd_sector.shape[0]
    amp = amplitudes.reshape(2, nblk, BLK).transpose(1, 0, 2).reshape(2 * nblk, BLK)
    pair = pair_occ.T
    owner, cd, ab = block_owner.T, cd_sector[None, :], ab_sector[None, :]
    outgoing, table, spread = pl.pallas_call(
        route_kernel,
        out_shape=(
            jax.ShapeDtypeStruct((512, BLK), BF16),
            pltpu.SMEM((8, BLK), jnp.int32),
            jax.ShapeDtypeStruct((8, BLK), F32),
        ),
        in_specs=[HBM] * 6,
        out_specs=(VMEM, SMEM, VMEM),
        scratch_shapes=[
            pltpu.SMEM(occ_irrep.shape, jnp.int32),
            pltpu.SMEM(pair.shape, jnp.int32),
            pltpu.VMEM(amp.shape, BF16),
            pltpu.VMEM(owner.shape, jnp.int32),
            pltpu.VMEM(cd.shape, jnp.int32),
            pltpu.VMEM(ab.shape, jnp.int32),
            pltpu.VMEM((8, BLK), jnp.int32),
            pltpu.SemaphoreType.DMA((6,)),
        ],
        compiler_params=pltpu.CompilerParams(vmem_limit_bytes=16 << 20),
        cost_estimate=pl.CostEstimate(flops=40 << 30, bytes_accessed=256 << 20, transcendentals=0),
        name="route",
    )(*hbm(occ_irrep, pair, amp, owner, cd, ab))
    incoming = lax.all_to_all(
        outgoing.reshape(32, 16, BLK), "vp", split_axis=0, concat_axis=0, tiled=True
    ).reshape(512, BLK)
    partial_value = pl.pallas_call(
        contract_kernel,
        out_shape=jax.ShapeDtypeStruct((1024, BLK), F32),
        in_specs=[SMEM, VMEM, VMEM],
        out_specs=VMEM,
        scratch_shapes=[pltpu.VMEM((512, BLK), F32)],
        compiler_params=pltpu.CompilerParams(vmem_limit_bytes=28 << 20),
        name="contract",
    )(table, incoming, pltpu.with_memory_space_constraint(integrals, pltpu.VMEM))
    gathered = lax.all_to_all(
        partial_value.reshape(128, 8, BLK), ("vp", "cd"), split_axis=0, concat_axis=0, tiled=True
    )
    return pl.pallas_call(
        collect_kernel,
        out_shape=jax.ShapeDtypeStruct((2, 2048), F32),
        in_specs=[VMEM, VMEM],
        out_specs=VMEM,
        compiler_params=pltpu.CompilerParams(vmem_limit_bytes=8 << 20),
        name="collect",
    )(spread, gathered)


def solution(mesh):
    return jax.shard_map(
        shards,
        mesh=mesh,
        in_specs=(P("vp", None), P(("vp", "cd"), None), P(), P(), P(), P(), P()),
        out_specs=P("vp", "cd"),
        check_vma=False,
    )
```

```python
import jax
import jax.numpy as jnp
from jax import lax
from jax.experimental import pallas as pl
from jax.experimental.pallas import tpu as pltpu
from jax.sharding import PartitionSpec as P

BLK = 128
F32 = jnp.float32
BF16 = jnp.bfloat16


def iota(shape, dim):
    return lax.broadcasted_iota(jnp.int32, shape, dim)


def ones_where(mask):
    return jnp.where(mask, 1.0, 0.0).astype(BF16)


def dot(a, b):
    return jnp.dot(a, b, preferred_element_type=F32)


def row_symmetry(occ, pair, row):
    return occ[pair[0, row]] ^ occ[pair[1, row]]


def fetch(sems, *pairs):
    copies = [pltpu.make_async_copy(src, dst, sems.at[i]) for i, (src, dst) in enumerate(pairs)]
    for copy in copies:
        copy.start()
    return copies


def route_kernel(
    occ_h, pair_h, amp_h, owner_h, cd_h, ab_h, out, table, spread,
    occ, pair, amp, owner, cd, ab, table_v, sems,
):
    copies = fetch(
        sems, (owner_h, owner), (cd_h, cd), (ab_h, ab), (occ_h, occ), (pair_h, pair), (amp_h, amp)
    )
    vp = (lax.axis_index("z") * 4 + lax.axis_index("x")) * 2 + lax.axis_index("c")
    y = lax.axis_index("y")
    nblk = owner.shape[1]
    nab = ab.shape[1]
    half_col = iota((nblk, 2 * nblk), 1) >> 1
    before = ones_where(iota((nblk, nblk), 0) < iota((nblk, nblk), 1))
    before2 = ones_where(iota((nblk, 2 * nblk), 0) < half_col)
    widen = ones_where(iota((nblk, 2 * nblk), 0) == half_col)
    j0 = iota((nab, nab), 0)
    j1 = iota((nab, nab), 1)
    within = ones_where((j0 < j1) & ((j0 >> 4) == (j1 >> 4)))
    for copy in copies[:5]:
        copy.wait()
    own = owner[...]
    cdf = cd[...].astype(F32)
    hot = own == vp * 4 + y
    rank = dot(jnp.broadcast_to(ones_where(hot), (16, nblk)), before)[:1]
    mine = jnp.where(hot, rank, -1.0)
    sym0 = row_symmetry(occ, pair, 2 * vp)
    sym1 = row_symmetry(occ, pair, 2 * vp + 1)
    row = iota((16, 1), 0)
    wanted = jnp.where(row < 8, row, jnp.where(row < 12, sym0, sym1))
    match = ab[...] == wanted
    order = dot(ones_where(match), within)
    source = iota((nab, BLK), 0)
    total = jnp.zeros((16, BLK), F32)
    for m in range(4):
        spot = iota((nab, BLK), 1) == (source >> 4) * 4 + m
        value = jnp.where(spot, source.astype(F32), 0.0).astype(BF16)
        total = total + dot(ones_where(match & (order == float(m))), value)
    slot = iota((8, 1), 0).astype(F32)
    sector = jnp.sum(jnp.where(mine == slot, cdf, 0.0), axis=1, keepdims=True)
    starts = jnp.zeros((8, BLK), F32)
    for t in range(4):
        starts = starts + jnp.where(sector == float(t), total[t:t + 1], 0.0)
    table_v[...] = starts.astype(jnp.int32)
    to_scalars = pltpu.make_async_copy(table_v, table, sems.at[0])
    to_scalars.start()
    hot32 = own == iota((32, nblk), 0) * 4 + y
    rank2 = dot(ones_where(hot32), before2)
    both = jnp.concatenate([own.astype(F32), cdf, jnp.zeros((14, nblk), F32)], axis=0)
    wide = dot(both.astype(BF16), widen)
    parity = iota((1, 2 * nblk), 1) & 1
    sym = jnp.where(parity == 0, sym0, sym1).astype(F32)
    ids = (iota((32, 1), 0) * 4 + y).astype(F32)
    keep = (wide[:1] == ids) & (wide[1:2] == sym)
    code = jnp.where(keep, rank2 * 2.0 + parity.astype(F32), -1.0)
    place = iota((32, 16, 2 * nblk), 1).astype(F32)
    select = ones_where(code[:, None, :] == place).reshape(512, 2 * nblk)
    shift = iota((nab, BLK), 0) == iota((nab, BLK), 1) + y * 16
    places = match & (order == (row & 3).astype(F32))
    spread[...] = dot(ones_where(places), ones_where(shift))[8:]
    copies[5].wait()
    out[...] = dot(select, amp[...]).astype(BF16)
    to_scalars.wait()


def contract_kernel(table, recv, integrals, own, other, wide):
    core = lax.axis_index("c")
    wide[...] = recv[...].astype(F32)
    slots = []
    for s in range(8):
        rows = [
            wide[pl.Slice(c * 16 + s * 2 + r, 16, stride=32), :]
            for c in (core, 1 - core)
            for r in range(2)
        ]
        slots.append(jnp.concatenate(rows, axis=0).astype(BF16))
    a = jnp.concatenate(slots, axis=1)
    for pair_at in range(8):
        columns = []
        for cb in (pair_at * 2, pair_at * 2 + 1):
            parts = []
            for s in range(8):
                start = pl.multiple_of(table[s, cb] * BLK, BLK)
                parts.append(integrals[s * BLK:(s + 1) * BLK, pl.ds(start, BLK)])
            columns.append(jnp.concatenate(parts, axis=0))
        result = dot(a, jnp.concatenate(columns, axis=1))
        for half in range(2):
            cb = pair_at * 2 + half
            for h, out in enumerate((own, other)):
                for r in range(2):
                    at = h * 32 + r * 16
                    out[pl.Slice((cb // 4) * 8 + r * 4 + cb % 4, 16, stride=32), :] = result[
                        at:at + 16, half * BLK:(half + 1) * BLK
                    ]


def collect_kernel(spread, recv, out):
    total = jnp.sum(recv[...], axis=0)
    places = spread[...]
    for j in range(16):
        line = jnp.where(places[:, j:j + 1] > 0.0, total, 0.0)
        out[0:1, j * BLK:(j + 1) * BLK] = jnp.sum(line[:4], axis=0, keepdims=True)
        out[1:2, j * BLK:(j + 1) * BLK] = jnp.sum(line[4:], axis=0, keepdims=True)


VMEM = pl.BlockSpec(memory_space=pltpu.VMEM)
SMEM = pl.BlockSpec(memory_space=pltpu.SMEM)
HBM = pl.BlockSpec(memory_space=pltpu.HBM)


def hbm(*arrays):
    return [pltpu.with_memory_space_constraint(a, pltpu.HBM) for a in arrays]


def shards(amplitudes, integrals, occ_irrep, pair_occ, cd_sector, ab_sector, block_owner):
    nblk = cd_sector.shape[0]
    amp = amplitudes.reshape(2, nblk, BLK).transpose(1, 0, 2).reshape(2 * nblk, BLK)
    pair = pair_occ.T
    owner, cd, ab = block_owner.T, cd_sector[None, :], ab_sector[None, :]
    outgoing, table, spread = pl.pallas_call(
        route_kernel,
        out_shape=(
            jax.ShapeDtypeStruct((512, BLK), BF16),
            pltpu.SMEM((8, BLK), jnp.int32),
            jax.ShapeDtypeStruct((8, BLK), F32),
        ),
        in_specs=[HBM] * 6,
        out_specs=(VMEM, SMEM, VMEM),
        scratch_shapes=[
            pltpu.SMEM(occ_irrep.shape, jnp.int32),
            pltpu.SMEM(pair.shape, jnp.int32),
            pltpu.VMEM(amp.shape, BF16),
            pltpu.VMEM(owner.shape, jnp.int32),
            pltpu.VMEM(cd.shape, jnp.int32),
            pltpu.VMEM(ab.shape, jnp.int32),
            pltpu.VMEM((8, BLK), jnp.int32),
            pltpu.SemaphoreType.DMA((6,)),
        ],
        compiler_params=pltpu.CompilerParams(vmem_limit_bytes=16 << 20),
        cost_estimate=pl.CostEstimate(flops=40 << 30, bytes_accessed=256 << 20, transcendentals=0),
        name="route",
    )(*hbm(occ_irrep, pair, amp, owner, cd, ab))
    incoming = lax.all_to_all(
        outgoing.reshape(32, 16, BLK), ("z", "x", "c"), split_axis=0, concat_axis=0, tiled=True
    ).reshape(512, BLK)
    own, other = pl.pallas_call(
        contract_kernel,
        out_shape=(jax.ShapeDtypeStruct((512, BLK), F32),) * 2,
        in_specs=[SMEM, VMEM, VMEM],
        out_specs=(VMEM, VMEM),
        scratch_shapes=[pltpu.VMEM((512, BLK), F32)],
        compiler_params=pltpu.CompilerParams(vmem_limit_bytes=28 << 20),
        name="contract",
    )(table, incoming, pltpu.with_memory_space_constraint(integrals, pltpu.VMEM))
    chip_sum = own + lax.ppermute(other, "c", [(0, 1), (1, 0)])
    gathered = lax.all_to_all(
        chip_sum.reshape(64, 8, BLK), ("z", "x", "y"), split_axis=0, concat_axis=0, tiled=True
    )
    return pl.pallas_call(
        collect_kernel,
        out_shape=jax.ShapeDtypeStruct((2, 2048), F32),
        in_specs=[VMEM, VMEM],
        out_specs=VMEM,
        compiler_params=pltpu.CompilerParams(vmem_limit_bytes=8 << 20),
        name="collect",
    )(spread, gathered)


def solution(mesh):
    grid = jax.sharding.Mesh(mesh.devices.reshape(4, 4, 2, 4), ("z", "x", "c", "y"))
    rows = ("z", "x", "c")
    return jax.shard_map(
        shards,
        mesh=grid,
        in_specs=(P(rows, None), P(rows + ("y",), None), P(), P(), P(), P(), P()),
        out_specs=P(rows, "y"),
        check_vma=False,
    )
```

```python
import jax
import jax.numpy as jnp
from jax import lax
from jax.experimental import pallas as pl
from jax.experimental.pallas import tpu as pltpu
from jax.sharding import PartitionSpec as P

BLK = 128
F32 = jnp.float32
BF16 = jnp.bfloat16


def iota(shape, dim):
    return lax.broadcasted_iota(jnp.int32, shape, dim)


def ones_where(mask):
    return jnp.where(mask, 1.0, 0.0).astype(BF16)


def dot(a, b):
    return jnp.dot(a, b, preferred_element_type=F32)


def row_symmetry(occ, pair, row):
    return occ[pair[0, row]] ^ occ[pair[1, row]]


def fetch(sems, *pairs):
    copies = [pltpu.make_async_copy(src, dst, sems.at[i]) for i, (src, dst) in enumerate(pairs)]
    for copy in copies:
        copy.start()
    return copies


def route_kernel(
    occ_h, pair_h, amp_h, owner_h, cd_h, ab_h, out, table, spread,
    occ, pair, amp, owner, cd, ab, ab_s, wide, sems,
):
    copies = fetch(
        sems, (owner_h, owner), (cd_h, cd), (ab_h, ab), (ab_h, ab_s), (occ_h, occ), (pair_h, pair), (amp_h, amp)
    )
    vp = (lax.axis_index("z") * 4 + lax.axis_index("x")) * 2 + lax.axis_index("c")
    y = lax.axis_index("y")
    nblk = owner.shape[1]
    nab = ab.shape[1]
    before = ones_where(iota((nblk, nblk), 0) < iota((nblk, nblk), 1))
    j0 = iota((nab, nab), 0)
    j1 = iota((nab, nab), 1)
    within = ones_where((j0 < j1) & ((j0 >> 4) == (j1 >> 4)))
    for copy in copies[:6]:
        copy.wait()
    sym0 = row_symmetry(occ, pair, 2 * vp)
    sym1 = row_symmetry(occ, pair, 2 * vp + 1)
    cdrow = cd[...]
    cdf = cdrow.astype(F32)
    prow = iota((48, 1), 0)
    hot = owner[...] == jnp.where(prow < 32, prow, vp) * 4 + y
    rank = dot(ones_where(hot), before)
    for panel in range(nab // 16):
        seen = jnp.int32(0)
        for j in range(panel * 16, panel * 16 + 16):
            t = ab_s[0, j]
            table[t, panel * 4 + ((seen >> (t * 8)) & 255)] = jnp.int32(j)
            seen = seen + (jnp.int32(1) << (t * 8))
    row = iota((16, 1), 0)
    wanted = jnp.where(row < 8, row, jnp.where(row < 12, sym0, sym1))
    match = ab[...] == wanted
    order = dot(ones_where(match), within)
    mine = jnp.where(hot[32:33], rank[32:33], -1.0)
    for s in range(8):
        sector = jnp.sum(jnp.where(mine == float(s), cdf, 0.0))
        table[4, s] = sector.astype(jnp.int32)
    place = iota((32, 8, nblk), 1).astype(F32)
    parts = []
    for r, sym in enumerate((sym0, sym1)):
        code = jnp.where(hot[:32] & (cdrow == sym), rank[:32], -1.0)
        select = ones_where(code[:, None, :] == place).reshape(256, nblk)
        parts.append(select)
    copies[-1].wait()
    wide[...] = amp[...].astype(F32)
    sums = [
        dot(parts[r], wide[pl.Slice(r, nblk, stride=2), :].astype(BF16)).reshape(32, 8, BLK)
        for r in range(2)
    ]
    out[...] = jnp.concatenate(sums, axis=1).reshape(512, BLK).astype(BF16)
    shift = iota((nab, BLK), 0) == iota((nab, BLK), 1) + y * 16
    places = match & (order == (row & 3).astype(F32))
    spread[...] = dot(ones_where(places), ones_where(shift))[8:]


def contract_kernel(table, recv, integrals, own, other, wide):
    core = lax.axis_index("c")
    wide[...] = recv[...].astype(F32)
    slots = []
    for s in range(8):
        rows = [
            wide[pl.Slice(c * 16 + r * 8 + s, 16, stride=32), :]
            for c in (core, 1 - core)
            for r in range(2)
        ]
        slots.append(jnp.concatenate(rows, axis=0).astype(BF16))
    a = jnp.concatenate(slots, axis=1)
    rows = [table[4, s] for s in range(8)]

    def block(s, cb):
        start = pl.multiple_of(table[rows[s], cb] * BLK, BLK)
        return integrals[s * BLK:(s + 1) * BLK, pl.ds(start, BLK)]

    for panels in range(2):
        result = jnp.zeros((64, 8 * BLK), F32)
        for s in range(0, 8, 2):
            weights = [
                jnp.concatenate([block(t, panels * 8 + i) for i in range(8)], axis=1)
                for t in (s, s + 1)
            ]
            result = result + dot(
                a[:, s * BLK:(s + 2) * BLK], jnp.concatenate(weights, axis=0)
            )
        for i in range(8):
            cb = panels * 8 + i
            for h, out in enumerate((own, other)):
                for r in range(2):
                    at = h * 32 + r * 16
                    out[pl.Slice((cb // 4) * 8 + r * 4 + cb % 4, 16, stride=32), :] = result[
                        at:at + 16, i * BLK:(i + 1) * BLK
                    ]


def collect_kernel(spread, recv, out):
    total = jnp.sum(recv[...], axis=0)
    places = spread[...]
    for j in range(16):
        line = jnp.where(places[:, j:j + 1] > 0.0, total, 0.0)
        out[0:1, j * BLK:(j + 1) * BLK] = jnp.sum(line[:4], axis=0, keepdims=True)
        out[1:2, j * BLK:(j + 1) * BLK] = jnp.sum(line[4:], axis=0, keepdims=True)


VMEM = pl.BlockSpec(memory_space=pltpu.VMEM)
SMEM = pl.BlockSpec(memory_space=pltpu.SMEM)
HBM = pl.BlockSpec(memory_space=pltpu.HBM)


def hbm(*arrays):
    return [pltpu.with_memory_space_constraint(a, pltpu.HBM) for a in arrays]


def shards(amplitudes, integrals, occ_irrep, pair_occ, cd_sector, ab_sector, block_owner):
    nblk = cd_sector.shape[0]
    amp = amplitudes.reshape(2, nblk, BLK).transpose(1, 0, 2).reshape(2 * nblk, BLK)
    pair = pair_occ.T
    owner, cd, ab = block_owner.T, cd_sector[None, :], ab_sector[None, :]
    outgoing, table, spread = pl.pallas_call(
        route_kernel,
        out_shape=(
            jax.ShapeDtypeStruct((512, BLK), BF16),
            pltpu.SMEM((8, BLK), jnp.int32),
            jax.ShapeDtypeStruct((8, BLK), F32),
        ),
        in_specs=[HBM] * 6,
        out_specs=(VMEM, SMEM, VMEM),
        scratch_shapes=[
            pltpu.SMEM(occ_irrep.shape, jnp.int32),
            pltpu.SMEM(pair.shape, jnp.int32),
            pltpu.VMEM(amp.shape, BF16),
            pltpu.VMEM(owner.shape, jnp.int32),
            pltpu.VMEM(cd.shape, jnp.int32),
            pltpu.VMEM(ab.shape, jnp.int32),
            pltpu.SMEM(ab.shape, jnp.int32),
            pltpu.VMEM(amp.shape, F32),
            pltpu.SemaphoreType.DMA((7,)),
        ],
        compiler_params=pltpu.CompilerParams(vmem_limit_bytes=16 << 20),
        cost_estimate=pl.CostEstimate(flops=40 << 30, bytes_accessed=256 << 20, transcendentals=0),
        name="route",
    )(*hbm(occ_irrep, pair, amp, owner, cd, ab))
    incoming = lax.all_to_all(
        outgoing.reshape(32, 16, BLK), ("z", "x", "c"), split_axis=0, concat_axis=0, tiled=True
    ).reshape(512, BLK)
    own, other = pl.pallas_call(
        contract_kernel,
        out_shape=(jax.ShapeDtypeStruct((512, BLK), F32),) * 2,
        in_specs=[SMEM, VMEM, VMEM],
        out_specs=(VMEM, VMEM),
        scratch_shapes=[pltpu.VMEM((512, BLK), F32)],
        compiler_params=pltpu.CompilerParams(vmem_limit_bytes=28 << 20),
        name="contract",
    )(table, incoming, pltpu.with_memory_space_constraint(integrals, pltpu.VMEM))
    chip_sum = own + lax.ppermute(other, "c", [(0, 1), (1, 0)])
    gathered = lax.all_to_all(
        chip_sum.reshape(64, 8, BLK), ("z", "x", "y"), split_axis=0, concat_axis=0, tiled=True
    )
    return pl.pallas_call(
        collect_kernel,
        out_shape=jax.ShapeDtypeStruct((2, 2048), F32),
        in_specs=[VMEM, VMEM],
        out_specs=VMEM,
        compiler_params=pltpu.CompilerParams(vmem_limit_bytes=8 << 20),
        name="collect",
    )(spread, gathered)


def solution(mesh):
    grid = jax.sharding.Mesh(mesh.devices.reshape(4, 4, 2, 4), ("z", "x", "c", "y"))
    rows = ("z", "x", "c")
    return jax.shard_map(
        shards,
        mesh=grid,
        in_specs=(P(rows, None), P(rows + ("y",), None), P(), P(), P(), P(), P()),
        out_specs=P(rows, "y"),
        check_vma=False,
    )
```

```python
import jax
import jax.numpy as jnp
from jax import lax
from jax.experimental import pallas as pl
from jax.experimental.pallas import tpu as pltpu
from jax.sharding import PartitionSpec as P

BLK = 128
F32 = jnp.float32
BF16 = jnp.bfloat16


def iota(shape, dim):
    return lax.broadcasted_iota(jnp.int32, shape, dim)


def ones_where(mask):
    return jnp.where(mask, 1.0, 0.0).astype(BF16)


def dot(a, b):
    return jnp.dot(a, b, preferred_element_type=F32)


def row_symmetry(occ, pair, row):
    return occ[pair[0, row]] ^ occ[pair[1, row]]


def fetch(sems, *pairs):
    copies = [pltpu.make_async_copy(src, dst, sems.at[i]) for i, (src, dst) in enumerate(pairs)]
    for copy in copies:
        copy.start()
    return copies


def route_kernel(
    occ_h, pair_h, amp_h, owner_h, cd_h, ab_h, out, table, spread,
    occ, pair, amp, owner, cd, ab, ab_s, wide, sems,
):
    copies = fetch(
        sems, (owner_h, owner), (cd_h, cd), (ab_h, ab), (ab_h, ab_s), (occ_h, occ), (pair_h, pair), (amp_h, amp)
    )
    vp = (lax.axis_index("z") * 4 + lax.axis_index("x")) * 2 + lax.axis_index("c")
    y = lax.axis_index("y")
    nblk = owner.shape[1]
    nab = ab.shape[1]
    before = ones_where(iota((nblk, nblk), 0) < iota((nblk, nblk), 1))
    j0 = iota((nab, nab), 0)
    j1 = iota((nab, nab), 1)
    within = ones_where((j0 < j1) & ((j0 >> 4) == (j1 >> 4)))
    for copy in copies[:6]:
        copy.wait()
    sym0 = row_symmetry(occ, pair, 2 * vp)
    sym1 = row_symmetry(occ, pair, 2 * vp + 1)
    cdrow = cd[...]
    cdf = cdrow.astype(F32)
    prow = iota((48, 1), 0)
    hot = owner[...] == jnp.where(prow < 32, (prow & 15) * 2 + (prow >> 4), vp) * 4 + y
    rank = dot(ones_where(hot), before)
    for panel in range(nab // 16):
        seen = jnp.int32(0)
        for j in range(panel * 16, panel * 16 + 16):
            t = ab_s[0, j]
            table[t, panel * 4 + ((seen >> (t * 8)) & 255)] = jnp.int32(j)
            seen = seen + (jnp.int32(1) << (t * 8))
    row = iota((16, 1), 0)
    wanted = jnp.where(row < 8, row, jnp.where(row < 12, sym0, sym1))
    match = ab[...] == wanted
    order = dot(ones_where(match), within)
    mine = jnp.where(hot[32:33], rank[32:33], -1.0)
    for s in range(8):
        sector = jnp.sum(jnp.where(mine == float(s), cdf, 0.0))
        table[4, s] = sector.astype(jnp.int32)
    place = iota((32, 8, nblk), 1).astype(F32)
    parts = []
    for r, sym in enumerate((sym0, sym1)):
        code = jnp.where(hot[:32] & (cdrow == sym), rank[:32], -1.0)
        select = ones_where(code[:, None, :] == place).reshape(256, nblk)
        parts.append(select)
    copies[-1].wait()
    wide[...] = amp[...].astype(F32)
    sums = [
        dot(parts[r], wide[pl.Slice(r, nblk, stride=2), :].astype(BF16)).reshape(32, 8, BLK)
        for r in range(2)
    ]
    out[...] = jnp.concatenate(sums, axis=1).reshape(512, BLK).astype(BF16)
    shift = iota((nab, BLK), 0) == iota((nab, BLK), 1) + y * 16
    places = match & (order == (row & 3).astype(F32))
    spread[...] = dot(ones_where(places), ones_where(shift))[8:]


def contract_kernel(table, recv, integrals, own, other, wide):
    core = lax.axis_index("c")
    for q in range(32):
        wide[q * 17:q * 17 + 16, :] = recv[q * 16:q * 16 + 16, :].astype(F32)
    slots = []
    for s in range(8):
        rows = [
            wide[pl.Slice(c * 272 + r * 8 + s, 16, stride=17), :]
            for c in (core, 1 - core)
            for r in range(2)
        ]
        slots.append(jnp.concatenate(rows, axis=0).astype(BF16))
    a = jnp.concatenate(slots, axis=1)
    rows = [table[4, s] for s in range(8)]

    def block(s, cb):
        start = pl.multiple_of(table[rows[s], cb] * BLK, BLK)
        return integrals[s * BLK:(s + 1) * BLK, pl.ds(start, BLK)]

    for panels in range(2):
        result = jnp.zeros((64, 8 * BLK), F32)
        for s in range(0, 8, 2):
            weights = [
                jnp.concatenate([block(t, panels * 8 + i) for i in range(8)], axis=1)
                for t in (s, s + 1)
            ]
            result = result + dot(
                a[:, s * BLK:(s + 2) * BLK], jnp.concatenate(weights, axis=0)
            )
        for i in range(8):
            cb = panels * 8 + i
            for h, out in enumerate((own, other)):
                for r in range(2):
                    at = h * 32 + r * 16
                    out[pl.Slice((cb // 4) * 128 + r * 4 + cb % 4, 16, stride=8), :] = result[
                        at:at + 16, i * BLK:(i + 1) * BLK
                    ]


def collect_kernel(spread, recv, out):
    total = jnp.sum(recv[...], axis=0)
    places = spread[...]
    for j in range(16):
        line = jnp.where(places[:, j:j + 1] > 0.0, total, 0.0)
        out[0:1, j * BLK:(j + 1) * BLK] = jnp.sum(line[:4], axis=0, keepdims=True)
        out[1:2, j * BLK:(j + 1) * BLK] = jnp.sum(line[4:], axis=0, keepdims=True)


VMEM = pl.BlockSpec(memory_space=pltpu.VMEM)
SMEM = pl.BlockSpec(memory_space=pltpu.SMEM)
HBM = pl.BlockSpec(memory_space=pltpu.HBM)


def hbm(*arrays):
    return [pltpu.with_memory_space_constraint(a, pltpu.HBM) for a in arrays]


def shards(amplitudes, integrals, occ_irrep, pair_occ, cd_sector, ab_sector, block_owner):
    nblk = cd_sector.shape[0]
    amp = amplitudes.reshape(2, nblk, BLK).transpose(1, 0, 2).reshape(2 * nblk, BLK)
    pair = pair_occ.T
    owner, cd, ab = block_owner.T, cd_sector[None, :], ab_sector[None, :]
    outgoing, table, spread = pl.pallas_call(
        route_kernel,
        out_shape=(
            jax.ShapeDtypeStruct((512, BLK), BF16),
            pltpu.SMEM((8, BLK), jnp.int32),
            jax.ShapeDtypeStruct((8, BLK), F32),
        ),
        in_specs=[HBM] * 6,
        out_specs=(VMEM, SMEM, VMEM),
        scratch_shapes=[
            pltpu.SMEM(occ_irrep.shape, jnp.int32),
            pltpu.SMEM(pair.shape, jnp.int32),
            pltpu.VMEM(amp.shape, BF16),
            pltpu.VMEM(owner.shape, jnp.int32),
            pltpu.VMEM(cd.shape, jnp.int32),
            pltpu.VMEM(ab.shape, jnp.int32),
            pltpu.SMEM(ab.shape, jnp.int32),
            pltpu.VMEM(amp.shape, F32),
            pltpu.SemaphoreType.DMA((7,)),
        ],
        compiler_params=pltpu.CompilerParams(vmem_limit_bytes=16 << 20),
        cost_estimate=pl.CostEstimate(flops=40 << 30, bytes_accessed=256 << 20, transcendentals=0),
        name="route",
    )(*hbm(occ_irrep, pair, amp, owner, cd, ab))
    incoming = lax.all_to_all(
        outgoing.reshape(32, 16, BLK), ("c", "z", "x"), split_axis=0, concat_axis=0, tiled=True
    ).reshape(512, BLK)
    own, other = pl.pallas_call(
        contract_kernel,
        out_shape=(jax.ShapeDtypeStruct((512, BLK), F32),) * 2,
        in_specs=[SMEM, VMEM, VMEM],
        out_specs=(VMEM, VMEM),
        scratch_shapes=[pltpu.VMEM((544, BLK), F32)],
        compiler_params=pltpu.CompilerParams(vmem_limit_bytes=28 << 20),
        name="contract",
    )(table, incoming, pltpu.with_memory_space_constraint(integrals, pltpu.VMEM))
    chip_sum = own + lax.ppermute(other, "c", [(0, 1), (1, 0)])
    gathered = lax.all_to_all(
        chip_sum.reshape(64, 8, BLK), ("y", "z", "x"), split_axis=0, concat_axis=0, tiled=True
    )
    return pl.pallas_call(
        collect_kernel,
        out_shape=jax.ShapeDtypeStruct((2, 2048), F32),
        in_specs=[VMEM, VMEM],
        out_specs=VMEM,
        compiler_params=pltpu.CompilerParams(vmem_limit_bytes=8 << 20),
        name="collect",
    )(spread, gathered)


def solution(mesh):
    grid = jax.sharding.Mesh(mesh.devices.reshape(4, 4, 2, 4), ("z", "x", "c", "y"))
    rows = ("z", "x", "c")
    return jax.shard_map(
        shards,
        mesh=grid,
        in_specs=(P(rows, None), P(rows + ("y",), None), P(), P(), P(), P(), P()),
        out_specs=P(rows, "y"),
        check_vma=False,
    )
```

```python
import jax
import jax.numpy as jnp
from jax import lax
from jax.experimental import pallas as pl
from jax.experimental.pallas import tpu as pltpu
from jax.sharding import PartitionSpec as P

BLK = 128
F32 = jnp.float32
BF16 = jnp.bfloat16


def iota(shape, dim):
    return lax.broadcasted_iota(jnp.int32, shape, dim)


def ones_where(mask):
    return jnp.where(mask, 1.0, 0.0).astype(BF16)


def dot(a, b):
    return jnp.dot(a, b, preferred_element_type=F32)


def row_symmetry(occ, pair, row):
    return occ[pair[0, row]] ^ occ[pair[1, row]]


def fetch(sems, *pairs):
    copies = [pltpu.make_async_copy(src, dst, sems.at[i]) for i, (src, dst) in enumerate(pairs)]
    for copy in copies:
        copy.start()
    return copies


def route_kernel(
    occ_h, pair_h, amp_h, owner_h, cd_h, ab_h, out, table, spread,
    occ, pair, amp, owner, cd, ab, ab_s, wide, sems,
):
    copies = fetch(
        sems, (owner_h, owner), (cd_h, cd), (ab_h, ab), (ab_h, ab_s), (occ_h, occ), (pair_h, pair), (amp_h, amp)
    )
    vp = (lax.axis_index("z") * 4 + lax.axis_index("x")) * 2 + lax.axis_index("c")
    y = lax.axis_index("y")
    nblk = owner.shape[1]
    nab = ab.shape[1]
    before = ones_where(iota((nblk, nblk), 0) < iota((nblk, nblk), 1))
    j0 = iota((nab, nab), 0)
    j1 = iota((nab, nab), 1)
    within = ones_where((j0 < j1) & ((j0 >> 4) == (j1 >> 4)))
    for copy in copies[:6]:
        copy.wait()
    sym0 = row_symmetry(occ, pair, 2 * vp)
    sym1 = row_symmetry(occ, pair, 2 * vp + 1)
    cdrow = cd[...]
    cdf = cdrow.astype(F32)
    prow = iota((48, 1), 0)
    hot = owner[...] == jnp.where(prow < 32, (prow & 15) * 2 + (prow >> 4), vp) * 4 + y
    rank = dot(ones_where(hot), before)
    row = iota((16, 1), 0)
    wanted = jnp.where(row < 8, row, jnp.where(row < 12, sym0, sym1))
    match = ab[...] == wanted
    order = dot(ones_where(match), within)
    place = iota((32, 8, nblk), 1).astype(F32)
    parts = []
    for r, sym in enumerate((sym0, sym1)):
        code = jnp.where(hot[:32] & (cdrow == sym), rank[:32], -1.0)
        select = ones_where(code[:, None, :] == place).reshape(256, nblk)
        parts.append(select)
    copies[-1].wait()
    wide[...] = amp[...].astype(F32)
    sums = [
        dot(parts[r], wide[pl.Slice(r, nblk, stride=2), :].astype(BF16)).reshape(32, 8, BLK)
        for r in range(2)
    ]
    out[...] = jnp.concatenate(sums, axis=1).reshape(512, BLK).astype(BF16)
    mine = jnp.where(hot[32:33], rank[32:33], -1.0)
    for s in range(8):
        sector = jnp.sum(jnp.where(mine == float(s), cdf, 0.0))
        table[4, s] = sector.astype(jnp.int32)
    for panel in range(nab // 16):
        seen = jnp.int32(0)
        for j in range(panel * 16, panel * 16 + 16):
            t = ab_s[0, j]
            table[t, panel * 4 + ((seen >> (t * 8)) & 255)] = jnp.int32(j)
            seen = seen + (jnp.int32(1) << (t * 8))
    shift = iota((nab, BLK), 0) == iota((nab, BLK), 1) + y * 16
    places = match & (order == (row & 3).astype(F32))
    spread[...] = dot(ones_where(places), ones_where(shift))[8:]


def contract_kernel(table, recv, integrals, own, other, wide):
    core = lax.axis_index("c")
    for q in range(32):
        wide[q * 17:q * 17 + 16, :] = recv[q * 16:q * 16 + 16, :].astype(F32)
    slots = []
    for s in range(8):
        rows = [
            wide[pl.Slice(c * 272 + r * 8 + s, 16, stride=17), :]
            for c in (core, 1 - core)
            for r in range(2)
        ]
        slots.append(jnp.concatenate(rows, axis=0).astype(BF16))
    a = jnp.concatenate(slots, axis=1)
    rows = [table[4, s] for s in range(8)]

    def block(s, cb):
        start = pl.multiple_of(table[rows[s], cb] * BLK, BLK)
        return integrals[s * BLK:(s + 1) * BLK, pl.ds(start, BLK)]

    for panels in range(2):
        result = jnp.zeros((64, 8 * BLK), F32)
        for s in range(0, 8, 2):
            weights = [
                jnp.concatenate([block(t, panels * 8 + i) for i in range(8)], axis=1)
                for t in (s, s + 1)
            ]
            result = result + dot(
                a[:, s * BLK:(s + 2) * BLK], jnp.concatenate(weights, axis=0)
            )
        for i in range(8):
            cb = panels * 8 + i
            for h, out in enumerate((own, other)):
                for r in range(2):
                    at = h * 32 + r * 16
                    out[pl.Slice((cb // 4) * 128 + r * 4 + cb % 4, 16, stride=8), :] = result[
                        at:at + 16, i * BLK:(i + 1) * BLK
                    ]


def collect_kernel(spread, recv, out):
    total = jnp.sum(recv[...], axis=0)
    places = spread[...]
    for j in range(16):
        line = jnp.where(places[:, j:j + 1] > 0.0, total, 0.0)
        out[0:1, j * BLK:(j + 1) * BLK] = jnp.sum(line[:4], axis=0, keepdims=True)
        out[1:2, j * BLK:(j + 1) * BLK] = jnp.sum(line[4:], axis=0, keepdims=True)


VMEM = pl.BlockSpec(memory_space=pltpu.VMEM)
SMEM = pl.BlockSpec(memory_space=pltpu.SMEM)
HBM = pl.BlockSpec(memory_space=pltpu.HBM)


def hbm(*arrays):
    return [pltpu.with_memory_space_constraint(a, pltpu.HBM) for a in arrays]


def shards(amplitudes, integrals, occ_irrep, pair_occ, cd_sector, ab_sector, block_owner):
    nblk = cd_sector.shape[0]
    amp = amplitudes.reshape(2, nblk, BLK).transpose(1, 0, 2).reshape(2 * nblk, BLK)
    pair = pair_occ.T
    owner, cd, ab = block_owner.T, cd_sector[None, :], ab_sector[None, :]
    outgoing, table, spread = pl.pallas_call(
        route_kernel,
        out_shape=(
            jax.ShapeDtypeStruct((512, BLK), BF16),
            pltpu.SMEM((8, BLK), jnp.int32),
            jax.ShapeDtypeStruct((8, BLK), F32),
        ),
        in_specs=[HBM] * 6,
        out_specs=(VMEM, SMEM, VMEM),
        scratch_shapes=[
            pltpu.SMEM(occ_irrep.shape, jnp.int32),
            pltpu.SMEM(pair.shape, jnp.int32),
            pltpu.VMEM(amp.shape, BF16),
            pltpu.VMEM(owner.shape, jnp.int32),
            pltpu.VMEM(cd.shape, jnp.int32),
            pltpu.VMEM(ab.shape, jnp.int32),
            pltpu.SMEM(ab.shape, jnp.int32),
            pltpu.VMEM(amp.shape, F32),
            pltpu.SemaphoreType.DMA((7,)),
        ],
        compiler_params=pltpu.CompilerParams(vmem_limit_bytes=16 << 20),
        cost_estimate=pl.CostEstimate(flops=40 << 30, bytes_accessed=256 << 20, transcendentals=0),
        name="route",
    )(*hbm(occ_irrep, pair, amp, owner, cd, ab))
    incoming = lax.all_to_all(
        outgoing.reshape(32, 16, BLK), ("c", "z", "x"), split_axis=0, concat_axis=0, tiled=True
    ).reshape(512, BLK)
    own, other = pl.pallas_call(
        contract_kernel,
        out_shape=(jax.ShapeDtypeStruct((512, BLK), F32),) * 2,
        in_specs=[SMEM, VMEM, VMEM],
        out_specs=(VMEM, VMEM),
        scratch_shapes=[pltpu.VMEM((544, BLK), F32)],
        compiler_params=pltpu.CompilerParams(vmem_limit_bytes=28 << 20),
        name="contract",
    )(table, incoming, pltpu.with_memory_space_constraint(integrals, pltpu.VMEM))
    chip_sum = own + lax.ppermute(other, "c", [(0, 1), (1, 0)])
    gathered = lax.all_to_all(
        chip_sum.reshape(64, 8, BLK), ("y", "z", "x"), split_axis=0, concat_axis=0, tiled=True
    )
    return pl.pallas_call(
        collect_kernel,
        out_shape=jax.ShapeDtypeStruct((2, 2048), F32),
        in_specs=[VMEM, VMEM],
        out_specs=VMEM,
        compiler_params=pltpu.CompilerParams(vmem_limit_bytes=8 << 20),
        name="collect",
    )(spread, gathered)


def solution(mesh):
    grid = jax.sharding.Mesh(mesh.devices.reshape(4, 4, 2, 4), ("z", "x", "c", "y"))
    rows = ("z", "x", "c")
    return jax.shard_map(
        shards,
        mesh=grid,
        in_specs=(P(rows, None), P(rows + ("y",), None), P(), P(), P(), P(), P()),
        out_specs=P(rows, "y"),
        check_vma=False,
    )
```

```python
import jax
import jax.numpy as jnp
from jax import lax
from jax.experimental import pallas as pl
from jax.experimental.pallas import tpu as pltpu
from jax.sharding import PartitionSpec as P

BLK = 128
F32 = jnp.float32
BF16 = jnp.bfloat16


def iota(shape, dim):
    return lax.broadcasted_iota(jnp.int32, shape, dim)


def ones_where(mask):
    return jnp.where(mask, 1.0, 0.0).astype(BF16)


def dot(a, b):
    return jnp.dot(a, b, preferred_element_type=F32)


def row_symmetry(occ, pair, row):
    return occ[pair[0, row]] ^ occ[pair[1, row]]


def fetch(sems, *pairs):
    copies = [pltpu.make_async_copy(src, dst, sems.at[i]) for i, (src, dst) in enumerate(pairs)]
    for copy in copies:
        copy.start()
    return copies


def route_kernel(
    occ_h, pair_h, amp_h, owner_h, cd_h, ab_h, out, table, spread,
    occ, pair, amp, owner, cd, ab, ab_s, wide, sems,
):
    copies = fetch(
        sems, (owner_h, owner), (cd_h, cd), (ab_h, ab), (ab_h, ab_s), (occ_h, occ), (pair_h, pair), (amp_h, amp)
    )
    vp = (lax.axis_index("z") * 4 + lax.axis_index("x")) * 2 + lax.axis_index("c")
    y = lax.axis_index("y")
    nblk = owner.shape[1]
    nab = ab.shape[1]
    before = ones_where(iota((nblk, nblk), 0) < iota((nblk, nblk), 1))
    j0 = iota((nab, nab), 0)
    j1 = iota((nab, nab), 1)
    within = ones_where((j0 < j1) & ((j0 >> 4) == (j1 >> 4)))
    for copy in copies[:6]:
        copy.wait()
    sym0 = row_symmetry(occ, pair, 2 * vp)
    sym1 = row_symmetry(occ, pair, 2 * vp + 1)
    cdrow = cd[...]
    cdf = cdrow.astype(F32)
    prow = iota((48, 1), 0)
    hot = owner[...] == jnp.where(prow < 32, (prow & 15) * 2 + (prow >> 4), vp) * 4 + y
    rank = dot(ones_where(hot), before)
    row = iota((16, 1), 0)
    wanted = jnp.where(row < 8, row, jnp.where(row < 12, sym0, sym1))
    match = ab[...] == wanted
    order = dot(ones_where(match), within)
    place = iota((32, 8, nblk), 1).astype(F32)
    parts = []
    for r, sym in enumerate((sym0, sym1)):
        code = jnp.where(hot[:32] & (cdrow == sym), rank[:32], -1.0)
        select = ones_where(code[:, None, :] == place).reshape(256, nblk)
        parts.append(select)
    copies[-1].wait()
    wide[...] = amp[...].astype(F32)
    sums = [
        dot(parts[r], wide[pl.Slice(r, nblk, stride=2), :].astype(BF16)).reshape(32, 8, BLK)
        for r in range(2)
    ]
    out[...] = jnp.concatenate(sums, axis=1).reshape(512, BLK).astype(BF16)
    mine = jnp.where(hot[32:33], rank[32:33], -1.0)
    for s in range(8):
        sector = jnp.sum(jnp.where(mine == float(s), cdf, 0.0))
        table[4, s] = sector.astype(jnp.int32)
    for panel in range(nab // 16):
        seen = jnp.int32(0)
        for j in range(panel * 16, panel * 16 + 16):
            t = ab_s[0, j]
            table[t, panel * 4 + ((seen >> (t * 8)) & 255)] = jnp.int32(j)
            seen = seen + (jnp.int32(1) << (t * 8))
    shift = iota((nab, BLK), 0) == iota((nab, BLK), 1) + y * 16
    places = match & (order == (row & 3).astype(F32))
    spread[...] = dot(ones_where(places), ones_where(shift))[8:]


def contract_kernel(table, recv, integrals, own, other, wide):
    core = lax.axis_index("c")
    for q in range(32):
        wide[q * 17:q * 17 + 16, :] = recv[q * 16:q * 16 + 16, :].astype(F32)
    slots = []
    for s in range(8):
        rows = [
            wide[pl.Slice(c * 272 + r * 8 + s, 16, stride=17), :]
            for c in (core, 1 - core)
            for r in range(2)
        ]
        slots.append(jnp.concatenate(rows, axis=0).astype(BF16))
    a = jnp.concatenate(slots, axis=1)
    rows = [table[4, s] for s in range(8)]

    def block(s, cb):
        start = pl.multiple_of(table[rows[s], cb] * BLK, BLK)
        return integrals[s * BLK:(s + 1) * BLK, pl.ds(start, BLK)]

    for panels in range(4):
        result = jnp.zeros((64, 4 * BLK), F32)
        for s in range(0, 8, 2):
            weights = [
                jnp.concatenate([block(t, panels * 4 + i) for i in range(4)], axis=1)
                for t in (s, s + 1)
            ]
            result = result + dot(
                a[:, s * BLK:(s + 2) * BLK], jnp.concatenate(weights, axis=0)
            )
        for i in range(4):
            cb = panels * 4 + i
            for h, out in enumerate((own, other)):
                for r in range(2):
                    at = h * 32 + r * 16
                    out[pl.Slice((cb // 4) * 128 + r * 4 + cb % 4, 16, stride=8), :] = result[
                        at:at + 16, i * BLK:(i + 1) * BLK
                    ]


def collect_kernel(spread, recv, out):
    parts = [jnp.sum(recv[k * 16:(k + 1) * 16], axis=0) for k in range(4)]
    total = (parts[0] + parts[1]) + (parts[2] + parts[3])
    places = spread[...]
    for j in range(16):
        line = jnp.where(places[:, j:j + 1] > 0.0, total, 0.0)
        out[0:1, j * BLK:(j + 1) * BLK] = jnp.sum(line[:4], axis=0, keepdims=True)
        out[1:2, j * BLK:(j + 1) * BLK] = jnp.sum(line[4:], axis=0, keepdims=True)


VMEM = pl.BlockSpec(memory_space=pltpu.VMEM)
SMEM = pl.BlockSpec(memory_space=pltpu.SMEM)
HBM = pl.BlockSpec(memory_space=pltpu.HBM)


def hbm(*arrays):
    return [pltpu.with_memory_space_constraint(a, pltpu.HBM) for a in arrays]


def shards(amplitudes, integrals, occ_irrep, pair_occ, cd_sector, ab_sector, block_owner):
    nblk = cd_sector.shape[0]
    amp = amplitudes.reshape(2, nblk, BLK).transpose(1, 0, 2).reshape(2 * nblk, BLK)
    pair = pair_occ.T
    owner, cd, ab = block_owner.T, cd_sector[None, :], ab_sector[None, :]
    outgoing, table, spread = pl.pallas_call(
        route_kernel,
        out_shape=(
            jax.ShapeDtypeStruct((512, BLK), BF16),
            pltpu.SMEM((8, BLK), jnp.int32),
            jax.ShapeDtypeStruct((8, BLK), F32),
        ),
        in_specs=[HBM] * 6,
        out_specs=(VMEM, SMEM, VMEM),
        scratch_shapes=[
            pltpu.SMEM(occ_irrep.shape, jnp.int32),
            pltpu.SMEM(pair.shape, jnp.int32),
            pltpu.VMEM(amp.shape, BF16),
            pltpu.VMEM(owner.shape, jnp.int32),
            pltpu.VMEM(cd.shape, jnp.int32),
            pltpu.VMEM(ab.shape, jnp.int32),
            pltpu.SMEM(ab.shape, jnp.int32),
            pltpu.VMEM(amp.shape, F32),
            pltpu.SemaphoreType.DMA((7,)),
        ],
        compiler_params=pltpu.CompilerParams(vmem_limit_bytes=16 << 20),
        cost_estimate=pl.CostEstimate(flops=40 << 30, bytes_accessed=256 << 20, transcendentals=0),
        name="route",
    )(*hbm(occ_irrep, pair, amp, owner, cd, ab))
    incoming = lax.all_to_all(
        outgoing.reshape(32, 16, BLK), ("c", "z", "x"), split_axis=0, concat_axis=0, tiled=True
    ).reshape(512, BLK)
    own, other = pl.pallas_call(
        contract_kernel,
        out_shape=(jax.ShapeDtypeStruct((512, BLK), F32),) * 2,
        in_specs=[SMEM, VMEM, VMEM],
        out_specs=(VMEM, VMEM),
        scratch_shapes=[pltpu.VMEM((544, BLK), F32)],
        compiler_params=pltpu.CompilerParams(vmem_limit_bytes=28 << 20),
        name="contract",
    )(table, incoming, pltpu.with_memory_space_constraint(integrals, pltpu.VMEM))
    chip_sum = own + lax.ppermute(other, "c", [(0, 1), (1, 0)])
    gathered = lax.all_to_all(
        chip_sum.reshape(64, 8, BLK), ("y", "z", "x"), split_axis=0, concat_axis=0, tiled=True
    )
    return pl.pallas_call(
        collect_kernel,
        out_shape=jax.ShapeDtypeStruct((2, 2048), F32),
        in_specs=[VMEM, VMEM],
        out_specs=VMEM,
        compiler_params=pltpu.CompilerParams(vmem_limit_bytes=8 << 20),
        name="collect",
    )(spread, gathered)


def solution(mesh):
    grid = jax.sharding.Mesh(mesh.devices.reshape(4, 4, 2, 4), ("z", "x", "c", "y"))
    rows = ("z", "x", "c")
    return jax.shard_map(
        shards,
        mesh=grid,
        in_specs=(P(rows, None), P(rows + ("y",), None), P(), P(), P(), P(), P()),
        out_specs=P(rows, "y"),
        check_vma=False,
    )
```

```python
import jax
import jax.numpy as jnp
from jax import lax
from jax.experimental import pallas as pl
from jax.experimental.pallas import tpu as pltpu
from jax.sharding import PartitionSpec as P

BLK = 128
F32 = jnp.float32
BF16 = jnp.bfloat16


def iota(shape, dim):
    return lax.broadcasted_iota(jnp.int32, shape, dim)


def ones_where(mask):
    return jnp.where(mask, 1.0, 0.0).astype(BF16)


def dot(a, b):
    return jnp.dot(a, b, preferred_element_type=F32)


def row_symmetry(occ, pair, row):
    return occ[pair[0, row]] ^ occ[pair[1, row]]


def fetch(sems, *pairs):
    copies = [pltpu.make_async_copy(src, dst, sems.at[i]) for i, (src, dst) in enumerate(pairs)]
    for copy in copies:
        copy.start()
    return copies


def route_kernel(
    occ_h, pair_h, amp_h, owner_h, cd_h, ab_h, out, table, spread,
    occ, pair, amp, owner, cd, ab, ab_s, wide, sems,
):
    copies = fetch(
        sems, (owner_h, owner), (cd_h, cd), (ab_h, ab), (ab_h, ab_s), (occ_h, occ), (pair_h, pair), (amp_h, amp)
    )
    vp = (lax.axis_index("z") * 4 + lax.axis_index("x")) * 2 + lax.axis_index("c")
    y = lax.axis_index("y")
    nblk = owner.shape[1]
    nab = ab.shape[1]
    before = ones_where(iota((nblk, nblk), 0) < iota((nblk, nblk), 1))
    j0 = iota((nab, nab), 0)
    j1 = iota((nab, nab), 1)
    within = ones_where((j0 < j1) & ((j0 >> 4) == (j1 >> 4)))
    for copy in copies[:6]:
        copy.wait()
    sym0 = row_symmetry(occ, pair, 2 * vp)
    sym1 = row_symmetry(occ, pair, 2 * vp + 1)
    cdrow = cd[...]
    cdf = cdrow.astype(F32)
    prow = iota((48, 1), 0)
    hot = owner[...] == jnp.where(prow < 32, (prow & 15) * 2 + (prow >> 4), vp) * 4 + y
    rank = dot(ones_where(hot), before)
    row = iota((16, 1), 0)
    wanted = jnp.where(row < 8, row, jnp.where(row < 12, sym0, sym1))
    match = ab[...] == wanted
    order = dot(ones_where(match), within)
    place = iota((32, 8, nblk), 1).astype(F32)
    parts = []
    for r, sym in enumerate((sym0, sym1)):
        code = jnp.where(hot[:32] & (cdrow == sym), rank[:32], -1.0)
        select = ones_where(code[:, None, :] == place).reshape(256, nblk)
        parts.append(select)
    copies[-1].wait()
    wide[...] = amp[...].astype(F32)
    sums = [
        dot(parts[r], wide[pl.Slice(r, nblk, stride=2), :].astype(BF16)).reshape(32, 8, BLK)
        for r in range(2)
    ]
    out[...] = jnp.concatenate(sums, axis=1).reshape(512, BLK).astype(BF16)
    mine = jnp.where(hot[32:33], rank[32:33], -1.0)
    for s in range(8):
        sector = jnp.sum(jnp.where(mine == float(s), cdf, 0.0))
        table[4, s] = sector.astype(jnp.int32)
    for panel in range(nab // 16):
        seen = jnp.int32(0)
        for j in range(panel * 16, panel * 16 + 16):
            t = ab_s[0, j]
            table[t, panel * 4 + ((seen >> (t * 8)) & 255)] = jnp.int32(j)
            seen = seen + (jnp.int32(1) << (t * 8))
    shift = iota((nab, BLK), 0) == iota((nab, BLK), 1) + y * 16
    places = match & (order == (row & 3).astype(F32))
    spread[...] = dot(ones_where(places), ones_where(shift))[8:]


def contract_kernel(table, recv, integrals, own, other, wide):
    core = lax.axis_index("c")
    for q in range(32):
        wide[q * 17:q * 17 + 16, :] = recv[q * 16:q * 16 + 16, :].astype(F32)
    slots = []
    for s in range(8):
        rows = [
            wide[pl.Slice(c * 272 + r * 8 + s, 16, stride=17), :]
            for c in (core, 1 - core)
            for r in range(2)
        ]
        slots.append(jnp.concatenate(rows, axis=0).astype(BF16))
    a = jnp.concatenate(slots, axis=1)
    rows = [table[4, s] for s in range(8)]

    def block(s, cb):
        start = pl.multiple_of(table[rows[s], cb] * BLK, BLK)
        return integrals[s * BLK:(s + 1) * BLK, pl.ds(start, BLK)]

    for panels in range(4):
        result = jnp.zeros((64, 4 * BLK), F32)
        for s in range(0, 8, 4):
            weights = [
                jnp.concatenate([block(t, panels * 4 + i) for i in range(4)], axis=1)
                for t in range(s, s + 4)
            ]
            result = result + dot(
                a[:, s * BLK:(s + 4) * BLK], jnp.concatenate(weights, axis=0)
            )
        for i in range(4):
            cb = panels * 4 + i
            for h, out in enumerate((own, other)):
                for r in range(2):
                    at = h * 32 + r * 16
                    out[pl.Slice((cb // 4) * 128 + r * 4 + cb % 4, 16, stride=8), :] = result[
                        at:at + 16, i * BLK:(i + 1) * BLK
                    ]


def collect_kernel(spread, recv, out):
    parts = [jnp.sum(recv[k * 16:(k + 1) * 16], axis=0) for k in range(4)]
    total = (parts[0] + parts[1]) + (parts[2] + parts[3])
    places = spread[...]
    for j in range(16):
        line = jnp.where(places[:, j:j + 1] > 0.0, total, 0.0)
        out[0:1, j * BLK:(j + 1) * BLK] = jnp.sum(line[:4], axis=0, keepdims=True)
        out[1:2, j * BLK:(j + 1) * BLK] = jnp.sum(line[4:], axis=0, keepdims=True)


VMEM = pl.BlockSpec(memory_space=pltpu.VMEM)
SMEM = pl.BlockSpec(memory_space=pltpu.SMEM)
HBM = pl.BlockSpec(memory_space=pltpu.HBM)


def hbm(*arrays):
    return [pltpu.with_memory_space_constraint(a, pltpu.HBM) for a in arrays]


def shards(amplitudes, integrals, occ_irrep, pair_occ, cd_sector, ab_sector, block_owner):
    nblk = cd_sector.shape[0]
    amp = amplitudes.reshape(2, nblk, BLK).transpose(1, 0, 2).reshape(2 * nblk, BLK)
    pair = pair_occ.T
    owner, cd, ab = block_owner.T, cd_sector[None, :], ab_sector[None, :]
    outgoing, table, spread = pl.pallas_call(
        route_kernel,
        out_shape=(
            jax.ShapeDtypeStruct((512, BLK), BF16),
            pltpu.SMEM((8, BLK), jnp.int32),
            jax.ShapeDtypeStruct((8, BLK), F32),
        ),
        in_specs=[HBM] * 6,
        out_specs=(VMEM, SMEM, VMEM),
        scratch_shapes=[
            pltpu.SMEM(occ_irrep.shape, jnp.int32),
            pltpu.SMEM(pair.shape, jnp.int32),
            pltpu.VMEM(amp.shape, BF16),
            pltpu.VMEM(owner.shape, jnp.int32),
            pltpu.VMEM(cd.shape, jnp.int32),
            pltpu.VMEM(ab.shape, jnp.int32),
            pltpu.SMEM(ab.shape, jnp.int32),
            pltpu.VMEM(amp.shape, F32),
            pltpu.SemaphoreType.DMA((7,)),
        ],
        compiler_params=pltpu.CompilerParams(vmem_limit_bytes=16 << 20),
        cost_estimate=pl.CostEstimate(flops=40 << 30, bytes_accessed=256 << 20, transcendentals=0),
        name="route",
    )(*hbm(occ_irrep, pair, amp, owner, cd, ab))
    incoming = lax.all_to_all(
        outgoing.reshape(32, 16, BLK), ("c", "z", "x"), split_axis=0, concat_axis=0, tiled=True
    ).reshape(512, BLK)
    own, other = pl.pallas_call(
        contract_kernel,
        out_shape=(jax.ShapeDtypeStruct((512, BLK), F32),) * 2,
        in_specs=[SMEM, VMEM, VMEM],
        out_specs=(VMEM, VMEM),
        scratch_shapes=[pltpu.VMEM((544, BLK), F32)],
        compiler_params=pltpu.CompilerParams(vmem_limit_bytes=28 << 20),
        name="contract",
    )(table, incoming, pltpu.with_memory_space_constraint(integrals, pltpu.VMEM))
    chip_sum = own + lax.ppermute(other, "c", [(0, 1), (1, 0)])
    gathered = lax.all_to_all(
        chip_sum.reshape(64, 8, BLK), ("y", "z", "x"), split_axis=0, concat_axis=0, tiled=True
    )
    return pl.pallas_call(
        collect_kernel,
        out_shape=jax.ShapeDtypeStruct((2, 2048), F32),
        in_specs=[VMEM, VMEM],
        out_specs=VMEM,
        compiler_params=pltpu.CompilerParams(vmem_limit_bytes=8 << 20),
        name="collect",
    )(spread, gathered)


def solution(mesh):
    grid = jax.sharding.Mesh(mesh.devices.reshape(4, 4, 2, 4), ("z", "x", "c", "y"))
    rows = ("z", "x", "c")
    return jax.shard_map(
        shards,
        mesh=grid,
        in_specs=(P(rows, None), P(rows + ("y",), None), P(), P(), P(), P(), P()),
        out_specs=P(rows, "y"),
        check_vma=False,
    )
```

```python
import jax
import jax.numpy as jnp
from jax import lax
from jax.experimental import pallas as pl
from jax.experimental.pallas import tpu as pltpu
from jax.sharding import PartitionSpec as P

BLK = 128
F32 = jnp.float32
BF16 = jnp.bfloat16


def iota(shape, dim):
    return lax.broadcasted_iota(jnp.int32, shape, dim)


def ones_where(mask):
    return jnp.where(mask, 1.0, 0.0).astype(BF16)


def dot(a, b):
    return jnp.dot(a, b, preferred_element_type=F32)


def row_symmetry(occ, pair, row):
    return occ[pair[0, row]] ^ occ[pair[1, row]]


def fetch(sems, *pairs):
    copies = [pltpu.make_async_copy(src, dst, sems.at[i]) for i, (src, dst) in enumerate(pairs)]
    for copy in copies:
        copy.start()
    return copies


def route_kernel(
    occ_h, pair_h, amp_h, owner_h, cd_h, ab_h, out, table, spread,
    occ, pair, amp, owner, cd, ab, ab_s, wide, sems,
):
    copies = fetch(
        sems, (owner_h, owner), (cd_h, cd), (ab_h, ab), (ab_h, ab_s), (occ_h, occ), (pair_h, pair), (amp_h, amp)
    )
    vp = (lax.axis_index("z") * 4 + lax.axis_index("x")) * 2 + lax.axis_index("c")
    y = lax.axis_index("y")
    nblk = owner.shape[1]
    nab = ab.shape[1]
    before = ones_where(iota((nblk, nblk), 0) < iota((nblk, nblk), 1))
    j0 = iota((nab, nab), 0)
    j1 = iota((nab, nab), 1)
    within = ones_where((j0 < j1) & ((j0 >> 4) == (j1 >> 4)))
    for copy in copies[:6]:
        copy.wait()
    sym0 = row_symmetry(occ, pair, 2 * vp)
    sym1 = row_symmetry(occ, pair, 2 * vp + 1)
    cdrow = cd[...]
    cdf = cdrow.astype(F32)
    prow = iota((48, 1), 0)
    hot = owner[...] == jnp.where(prow < 32, (prow & 15) * 2 + (prow >> 4), vp) * 4 + y
    rank = dot(ones_where(hot), before)
    row = iota((16, 1), 0)
    wanted = jnp.where(row < 8, row, jnp.where(row < 12, sym0, sym1))
    match = ab[...] == wanted
    order = dot(ones_where(match), within)
    place = iota((32, 8, nblk), 1).astype(F32)
    parts = []
    for r, sym in enumerate((sym0, sym1)):
        code = jnp.where(hot[:32] & (cdrow == sym), rank[:32], -1.0)
        select = ones_where(code[:, None, :] == place).reshape(256, nblk)
        parts.append(select)
    copies[-1].wait()
    wide[...] = amp[...].astype(F32)
    sums = [
        dot(parts[r], wide[pl.Slice(r, nblk, stride=2), :].astype(BF16)).reshape(32, 8, BLK)
        for r in range(2)
    ]
    out[...] = jnp.concatenate(sums, axis=1).reshape(512, BLK).astype(BF16)
    mine = jnp.where(hot[32:33], rank[32:33], -1.0)
    for s in range(8):
        sector = jnp.sum(jnp.where(mine == float(s), cdf, 0.0))
        table[4, s] = sector.astype(jnp.int32)
    for panel in range(nab // 16):
        seen = jnp.int32(0)
        for j in range(panel * 16, panel * 16 + 16):
            t = ab_s[0, j]
            table[t, panel * 4 + ((seen >> (t * 8)) & 255)] = jnp.int32(j)
            seen = seen + (jnp.int32(1) << (t * 8))
    shift = iota((nab, BLK), 0) == iota((nab, BLK), 1) + y * 16
    places = match & (order == (row & 3).astype(F32))
    spread[...] = dot(ones_where(places), ones_where(shift))[8:]


def contract_kernel(table, recv, integrals, own, other, wide):
    core = lax.axis_index("c")
    for q in range(32):
        wide[q * 17:q * 17 + 16, :] = recv[q * 16:q * 16 + 16, :].astype(F32)
    slots = []
    for s in range(8):
        rows = [
            wide[pl.Slice(c * 272 + r * 8 + s, 16, stride=17), :]
            for c in (core, 1 - core)
            for r in range(2)
        ]
        slots.append(jnp.concatenate(rows, axis=0).astype(BF16))
    a = jnp.concatenate(slots, axis=1)
    rows = [table[4, s] for s in range(8)]

    def block(s, cb):
        start = pl.multiple_of(table[rows[s], cb] * BLK, BLK)
        return integrals[s * BLK:(s + 1) * BLK, pl.ds(start, BLK)]

    for panels in range(4):
        result = jnp.zeros((64, 4 * BLK), F32)
        for s in range(0, 8, 8):
            weights = [
                jnp.concatenate([block(t, panels * 4 + i) for i in range(4)], axis=1)
                for t in range(s, s + 8)
            ]
            result = result + dot(
                a[:, s * BLK:(s + 8) * BLK], jnp.concatenate(weights, axis=0)
            )
        for i in range(4):
            cb = panels * 4 + i
            for h, out in enumerate((own, other)):
                for r in range(2):
                    at = h * 32 + r * 16
                    out[pl.Slice((cb // 4) * 128 + r * 4 + cb % 4, 16, stride=8), :] = result[
                        at:at + 16, i * BLK:(i + 1) * BLK
                    ]


def collect_kernel(spread, recv, out):
    parts = [jnp.sum(recv[k * 16:(k + 1) * 16], axis=0) for k in range(4)]
    total = (parts[0] + parts[1]) + (parts[2] + parts[3])
    places = spread[...]
    for j in range(16):
        line = jnp.where(places[:, j:j + 1] > 0.0, total, 0.0)
        out[0:1, j * BLK:(j + 1) * BLK] = jnp.sum(line[:4], axis=0, keepdims=True)
        out[1:2, j * BLK:(j + 1) * BLK] = jnp.sum(line[4:], axis=0, keepdims=True)


VMEM = pl.BlockSpec(memory_space=pltpu.VMEM)
SMEM = pl.BlockSpec(memory_space=pltpu.SMEM)
HBM = pl.BlockSpec(memory_space=pltpu.HBM)


def hbm(*arrays):
    return [pltpu.with_memory_space_constraint(a, pltpu.HBM) for a in arrays]


def shards(amplitudes, integrals, occ_irrep, pair_occ, cd_sector, ab_sector, block_owner):
    nblk = cd_sector.shape[0]
    amp = amplitudes.reshape(2, nblk, BLK).transpose(1, 0, 2).reshape(2 * nblk, BLK)
    pair = pair_occ.T
    owner, cd, ab = block_owner.T, cd_sector[None, :], ab_sector[None, :]
    outgoing, table, spread = pl.pallas_call(
        route_kernel,
        out_shape=(
            jax.ShapeDtypeStruct((512, BLK), BF16),
            pltpu.SMEM((8, BLK), jnp.int32),
            jax.ShapeDtypeStruct((8, BLK), F32),
        ),
        in_specs=[HBM] * 6,
        out_specs=(VMEM, SMEM, VMEM),
        scratch_shapes=[
            pltpu.SMEM(occ_irrep.shape, jnp.int32),
            pltpu.SMEM(pair.shape, jnp.int32),
            pltpu.VMEM(amp.shape, BF16),
            pltpu.VMEM(owner.shape, jnp.int32),
            pltpu.VMEM(cd.shape, jnp.int32),
            pltpu.VMEM(ab.shape, jnp.int32),
            pltpu.SMEM(ab.shape, jnp.int32),
            pltpu.VMEM(amp.shape, F32),
            pltpu.SemaphoreType.DMA((7,)),
        ],
        compiler_params=pltpu.CompilerParams(vmem_limit_bytes=16 << 20),
        cost_estimate=pl.CostEstimate(flops=40 << 30, bytes_accessed=256 << 20, transcendentals=0),
        name="route",
    )(*hbm(occ_irrep, pair, amp, owner, cd, ab))
    incoming = lax.all_to_all(
        outgoing.reshape(32, 16, BLK), ("c", "z", "x"), split_axis=0, concat_axis=0, tiled=True
    ).reshape(512, BLK)
    own, other = pl.pallas_call(
        contract_kernel,
        out_shape=(jax.ShapeDtypeStruct((512, BLK), F32),) * 2,
        in_specs=[SMEM, VMEM, VMEM],
        out_specs=(VMEM, VMEM),
        scratch_shapes=[pltpu.VMEM((544, BLK), F32)],
        compiler_params=pltpu.CompilerParams(vmem_limit_bytes=28 << 20),
        name="contract",
    )(table, incoming, pltpu.with_memory_space_constraint(integrals, pltpu.VMEM))
    chip_sum = own + lax.ppermute(other, "c", [(0, 1), (1, 0)])
    gathered = lax.all_to_all(
        chip_sum.reshape(64, 8, BLK), ("y", "z", "x"), split_axis=0, concat_axis=0, tiled=True
    )
    return pl.pallas_call(
        collect_kernel,
        out_shape=jax.ShapeDtypeStruct((2, 2048), F32),
        in_specs=[VMEM, VMEM],
        out_specs=VMEM,
        compiler_params=pltpu.CompilerParams(vmem_limit_bytes=8 << 20),
        name="collect",
    )(spread, gathered)


def solution(mesh):
    grid = jax.sharding.Mesh(mesh.devices.reshape(4, 4, 2, 4), ("z", "x", "c", "y"))
    rows = ("z", "x", "c")
    return jax.shard_map(
        shards,
        mesh=grid,
        in_specs=(P(rows, None), P(rows + ("y",), None), P(), P(), P(), P(), P()),
        out_specs=P(rows, "y"),
        check_vma=False,
    )
```
